128 devices in a mesh: leaf: 4 (over x), box: 32 (over y, z, core).
Axes of the slice: x: 4, y: 4, z: 4, core: 2. Of those that a mesh axis runs over, the one named last changes fastest.
Arguments:
- charges: bfloat16 [8192, 32, 256], P(('leaf', 'box')), may hold values from -6 to 6
- counts: int32 [8192], P(('leaf', 'box')), may hold values from 32 to 256
- leaf_basis: bfloat16 [8192, 64, 256], P(('leaf', 'box')), may hold values from -0.375 to 0.375
- out_basis: bfloat16 [8192, 64, 256], P(('leaf', 'box')), may hold values from -0.75 to 0.75
- leaf_transfer: bfloat16 [8192, 64, 64], P(('leaf', 'box')), may hold values from -0.25 to 0.25
- leaf_descend: bfloat16 [8192, 64, 64], P(('leaf', 'box')), may hold values from -0.75 to 0.75
- parent_transfer: bfloat16 [1024, 64, 64], P(('leaf', 'box')), may hold values from -0.25 to 0.25
- parent_descend: bfloat16 [1024, 64, 64], P(('leaf', 'box')), may hold values from -0.75 to 0.75
- leaf_coupling: bfloat16 [8192, 16, 64, 64], P(('leaf', 'box')), may hold values from -0.1875 to 0.1875
- far_owner: int32 [8192, 16], P(('leaf', 'box')), may hold values from 0 to 31, as said below
- far_local: int32 [8192, 16], P(('leaf', 'box')), may hold values from 0 to 63
- parent_coupling: bfloat16 [1024, 16, 64, 64], P(('leaf', 'box')), may hold values from -0.1875 to 0.1875
- parent_owner: int32 [1024, 16], P(('leaf', 'box')), may hold values from 0 to 31
- parent_index: int32 [1024, 16], P(('leaf', 'box')), may hold values from 0 to 7
- top_coupling: bfloat16 [128, 16, 64, 64], P(('leaf', 'box')), may hold values from -0.1875 to 0.1875
- top_source: int32 [128, 16], P(('leaf', 'box')), may hold values from 0 to 127
Outputs:
- potential: bfloat16 [8192, 32, 256], P(('leaf', 'box'))
The draws below stay inside these ranges and needn't reach their ends.
Inputs may be any that keep to these rules, and one draw needn't show every extreme that they name: `far_owner`: among the 1024 entries of the rows of one device, at most 48 name the same device, and one device is named by exactly 48 entries of every device's rows.
All inputs are finite; a program needn't handle non-finite values.
Results may differ from the reference program's by a relative error of at most 0.014.
Values may be sent and summed in bfloat16 or wider, within the bound.
No kernel may reach another device: no remote copies, remote signals or barrier semaphores. Data moves between devices by JAX's collectives and lax.ppermute only.
A program may use at most 128 MiB of HBM per device.

```python
import jax
import jax.numpy as jnp
from jax import lax

POINTS = 256
VECTORS = 32
SKELETON = 64
LIST_SLOTS = 16
PARENT_DEV = 8
LEAF_DEV = 64
LEAVES = 8192
PARENTS = 1024
TOP_BOXES = 128
N_LEAF = 4
N_BOX = 32


def draw_far_owner(key, part):
    key = jax.random.fold_in(key, 11)
    entries = LEAF_DEV * LIST_SLOTS
    devices = N_LEAF * N_BOX
    capacity = 3 * entries // (2 * N_BOX)
    busiest = jax.random.randint(jax.random.fold_in(key, 1), (), 0, N_BOX)
    position = jnp.arange(entries, dtype=jnp.int32)
    spread = 1 + jnp.maximum(position - capacity, 0) % (N_BOX - 1)
    offset = jnp.where(position < capacity, 0, spread)
    owner_base = (busiest + offset) % N_BOX

    def device_block(device_index):
        shuffle = jax.random.permutation(jax.random.fold_in(key, 100 + device_index), entries)
        return owner_base[shuffle]
    blocks = jax.vmap(device_block)(jnp.arange(devices, dtype=jnp.int32))
    return blocks.reshape(devices * LEAF_DEV, LIST_SLOTS).astype(jnp.int32)


def touch_ends(drawn, rng, least, top_value):
    longest = drawn.shape.index(max(drawn.shape))
    spots = []
    for shift in (0, 1):
        where = [jax.random.randint(jax.random.fold_in(rng, axis), (), 0, length) for axis, length in enumerate(drawn.shape)]
        where[longest] = (where[longest] + shift) % drawn.shape[longest]
        spots.append(tuple(where))
    return drawn.at[spots[0]].set(least).at[spots[1]].set(top_value)


def block_levels(stream_key, extent, cuts, smallest, top_value):
    def one(dim, parts):
        heights = jax.random.uniform(jax.random.fold_in(jax.random.fold_in(stream_key, 6), dim), (parts,), jnp.float32, smallest / len(cuts), top_value / len(cuts))
        return jnp.repeat(jnp.exp(heights), extent[dim] // parts).reshape((-1,) + (1,) * (len(extent) - dim - 1))

    level = one(*cuts[0])
    for cut in cuts[1:]:
        level = level * one(*cut)
    return level


def gaussian(rng, extent, width, reach, shards=(), kind=jnp.bfloat16):
    factor_of = block_levels(rng, extent, shards, -0.22, 0.18) if shards else 1.0
    values = jax.random.normal(rng, extent, jnp.float32) * width * factor_of
    return jnp.minimum(jnp.maximum(values, -reach), reach).astype(kind)


def setup_inputs(seed: int = 0) -> dict:
    key_of = jax.random.split(jax.random.key(seed), 17)
    charges = gaussian(key_of[0], (LEAVES, VECTORS, POINTS), 1.0, 6.0, ((0, 128),))
    counts = touch_ends(jax.random.randint(key_of[1], (LEAVES,), POINTS // 8, POINTS + 1), jax.random.fold_in(key_of[1], 1), POINTS // 8, POINTS).astype(jnp.int32)
    leaf_basis = gaussian(key_of[2], (LEAVES, SKELETON, POINTS), POINTS ** -0.5, 0.375, ((0, 128),))
    out_basis = gaussian(key_of[3], (LEAVES, SKELETON, POINTS), SKELETON ** -0.5, 0.75, ((0, 128),))
    leaf_transfer = gaussian(key_of[4], (LEAVES, SKELETON, SKELETON), (8 * SKELETON) ** -0.5, 0.25, ((0, 128),))
    leaf_descend = gaussian(key_of[5], (LEAVES, SKELETON, SKELETON), SKELETON ** -0.5, 0.75, ((0, 128),))
    parent_transfer = gaussian(key_of[6], (PARENTS, SKELETON, SKELETON), (8 * SKELETON) ** -0.5, 0.25, ((0, 128),))
    parent_descend = gaussian(key_of[7], (PARENTS, SKELETON, SKELETON), SKELETON ** -0.5, 0.75, ((0, 128),))
    leaf_coupling = gaussian(key_of[8], (LEAVES, LIST_SLOTS, SKELETON, SKELETON), (LIST_SLOTS * SKELETON) ** -0.5, 0.1875, ((0, 128),))
    far_owner = draw_far_owner(jax.random.fold_in(key_of[16], 71), 0)
    far_local = touch_ends(jax.random.randint(key_of[10], (LEAVES, LIST_SLOTS), 0, LEAF_DEV), jax.random.fold_in(key_of[10], 1), 0, LEAF_DEV - 1).astype(jnp.int32)
    parent_coupling = gaussian(key_of[11], (PARENTS, LIST_SLOTS, SKELETON, SKELETON), (LIST_SLOTS * SKELETON) ** -0.5, 0.1875, ((0, 128),))
    parent_owner = touch_ends(jax.random.randint(key_of[12], (PARENTS, LIST_SLOTS), 0, N_BOX), jax.random.fold_in(key_of[12], 1), 0, N_BOX - 1).astype(jnp.int32)
    parent_index = touch_ends(jax.random.randint(key_of[13], (PARENTS, LIST_SLOTS), 0, PARENT_DEV), jax.random.fold_in(key_of[13], 1), 0, PARENT_DEV - 1).astype(jnp.int32)
    top_coupling = gaussian(key_of[14], (TOP_BOXES, LIST_SLOTS, SKELETON, SKELETON), (LIST_SLOTS * SKELETON) ** -0.5, 0.1875, ((0, 128),))
    top_source = touch_ends(jax.random.randint(key_of[15], (TOP_BOXES, LIST_SLOTS), 0, TOP_BOXES), jax.random.fold_in(key_of[15], 1), 0, TOP_BOXES - 1).astype(jnp.int32)
    return {"charges": charges, "counts": counts, "leaf_basis": leaf_basis, "out_basis": out_basis, "leaf_transfer": leaf_transfer, "leaf_descend": leaf_descend, "parent_transfer": parent_transfer, "parent_descend": parent_descend, "leaf_coupling": leaf_coupling, "far_owner": far_owner, "far_local": far_local, "parent_coupling": parent_coupling, "parent_owner": parent_owner, "parent_index": parent_index, "top_coupling": top_coupling, "top_source": top_source}


def couple(coeffs, source_rows, couplings, groups):
    grouped_rows = source_rows.reshape(groups, -1, LIST_SLOTS)
    grouped_mats = couplings.reshape(groups, -1, LIST_SLOTS, SKELETON, SKELETON)

    def block_product(pieces):
        chosen, matrices = pieces
        picked = coeffs[chosen].astype(jnp.float32)
        return jnp.einsum('tjrk,tjkq->trq', picked, matrices.astype(jnp.float32))

    result = lax.map(block_product, (grouped_rows, grouped_mats))
    return result.reshape(-1, VECTORS, SKELETON)


def ascend(coeffs, transfer):
    groups = coeffs.shape[0] // 8
    grouped = coeffs.reshape(groups, 8, VECTORS, SKELETON).astype(jnp.float32)
    matrices = transfer.reshape(groups, 8, SKELETON, SKELETON).astype(jnp.float32)
    return jnp.einsum('pcrk,pckq->prq', grouped, matrices)


def descend(field, matrices):
    groups = field.shape[0]
    grouped = matrices.reshape(groups, 8, SKELETON, SKELETON).astype(jnp.float32)
    result = jnp.einsum('prq,pcqk->pcrk', field.astype(jnp.float32), grouped)
    return result.reshape(groups * 8, VECTORS, SKELETON)


def reference(charges, counts, leaf_basis, out_basis, leaf_transfer, leaf_descend, parent_transfer, parent_descend, leaf_coupling, far_owner, far_local, parent_coupling, parent_owner, parent_index, top_coupling, top_source):
    devices = N_LEAF * N_BOX
    inside = jnp.arange(POINTS, dtype=jnp.int32)[None, None, :] < counts[:, None, None]
    masked = jnp.where(inside, charges, jnp.zeros_like(charges))
    leaf_coeff = jnp.einsum('brp,bkp->brk', masked.astype(jnp.float32), leaf_basis.astype(jnp.float32)).astype(jnp.bfloat16)
    parent_coeff = ascend(leaf_coeff, leaf_transfer).astype(jnp.bfloat16)
    top_coeff = ascend(parent_coeff, parent_transfer).astype(jnp.bfloat16)
    top_field = couple(top_coeff, top_source, top_coupling, devices).astype(jnp.bfloat16)
    parent_ids = jnp.arange(PARENTS, dtype=jnp.int32)
    parent_base = (parent_ids // (N_BOX * PARENT_DEV)) * N_BOX
    parent_rows = ((parent_base[:, None] + parent_owner) * PARENT_DEV + parent_index).astype(jnp.int32)
    parent_field = (couple(parent_coeff, parent_rows, parent_coupling, devices) + descend(top_field, parent_descend)).astype(jnp.bfloat16)
    leaf_ids = jnp.arange(LEAVES, dtype=jnp.int32)
    leaf_base = (leaf_ids // (N_BOX * LEAF_DEV)) * N_BOX
    leaf_rows = ((leaf_base[:, None] + far_owner) * LEAF_DEV + far_local).astype(jnp.int32)
    leaf_field = (couple(leaf_coeff, leaf_rows, leaf_coupling, devices) + descend(parent_field, leaf_descend)).astype(jnp.bfloat16)
    values = jnp.einsum('brk,bkp->brp', leaf_field.astype(jnp.float32), out_basis.astype(jnp.float32))
    return jnp.where(inside, values, jnp.zeros_like(values)).astype(jnp.bfloat16)
```

```python
import functools

import jax
import jax.numpy as jnp
from jax import lax
from jax.experimental import pallas as pl
from jax.experimental.pallas import tpu as pltpu
from jax.sharding import Mesh
from jax.sharding import PartitionSpec as P

BF16 = jnp.bfloat16
F32 = jnp.float32
LEAF, PARENT = 64, 8
ROWS = LEAF + PARENT + 1
CUT = 37
NT = (((1,), (1,)), ((), ()))
MIB = 1 << 20


def dot(a, b):
    return jnp.dot(a, b, preferred_element_type=F32)


def pack(c):
    return jnp.concatenate([c[:16], c[16:]], axis=1)


def up_kernel(per, counts, charges, basis, transfer, parent_transfer, out, top):
    step = pl.program_id(0)
    column = lax.broadcasted_iota(jnp.int32, (32, 256), 1)

    @pl.when(step == 0)
    def _():
        top[...] = jnp.zeros_like(top)

    for p in range(per):
        total = jnp.zeros((32, 64), F32)
        for i in range(8):
            b = p * 8 + i
            live = column < counts[step * per * 8 + b]
            masked = jnp.where(live, charges[b], jnp.zeros((32, 256), BF16))
            coeff = lax.dot_general(masked, basis[b], NT, preferred_element_type=F32).astype(BF16)
            out[step * per * 8 + b] = pack(coeff)
            total += dot(coeff, transfer[b])
        parent = total.astype(BF16)
        out[LEAF + step * per + p] = pack(parent)
        top[...] += dot(parent, parent_transfer[p])

    @pl.when(step == pl.num_programs(0) - 1)
    def _():
        out[ROWS - 1] = pack(top[...].astype(BF16))


def up(counts, charges, basis, transfer, parent_transfer):
    per = 2
    steps = PARENT // per
    block = lambda *s: pl.BlockSpec(s, lambda i: (i,) + (0,) * (len(s) - 1))
    return pl.pallas_call(
        functools.partial(up_kernel, per),
        grid=(steps,),
        in_specs=[
            pl.BlockSpec(memory_space=pltpu.SMEM),
            block(8 * per, 32, 256),
            block(8 * per, 64, 256),
            block(8 * per, 64, 64),
            block(per, 64, 64),
        ],
        out_specs=pl.BlockSpec((ROWS, 16, 128), lambda i: (0, 0, 0)),
        out_shape=jax.ShapeDtypeStruct((ROWS, 16, 128), BF16),
        scratch_shapes=[pltpu.VMEM((32, 64), F32)],
        compiler_params=pltpu.CompilerParams(vmem_limit_bytes=16 * MIB),
        cost_estimate=pl.CostEstimate(flops=2 * 64 * 32 * 64 * 320, bytes_accessed=5 * MIB, transcendentals=0),
        name="up",
    )(counts, charges, basis, transfer, parent_transfer)


def pairs(second, mask):
    out = []
    for y in range(4):
        for z in range(4):
            for c in range(2):
                along_y = (c == 0) != second
                ty, tz = (y ^ mask, z) if along_y else (y, z ^ mask)
                out.append(((y * 4 + z) * 2 + c, (ty * 4 + tz) * 2 + c))
    return out


def send(x, second, mask):
    return lax.ppermute(x, ("y", "z", "c"), pairs(second, mask))


def other_core(x):
    return lax.ppermute(x, "c", [(0, 1), (1, 0)])


def gather_pieces(s):
    s = s[None]
    full, low, high = (0, ROWS), (0, CUT), (CUT, ROWS - CUT)
    a, b = send(s, False, 1), send(s, False, 3)
    va1, vb1 = send(s, True, 1), send(s, True, 3)
    o_low = send(a[:, :CUT], False, 3)
    o_high = send(b[:, CUT:], False, 1)
    t2 = jnp.concatenate([a, b])
    va2, vb2 = send(t2, True, 1), send(t2, True, 3)
    o = jnp.concatenate([o_low, o_high], axis=1)
    va3, vb3 = send(o, True, 1), send(o, True, 3)
    f1_low = send(va1[:, :CUT], True, 3)
    f1_high = send(vb1[:, CUT:], True, 1)
    f2_a = send(va2[:1], True, 3)
    f2_b = send(vb2[1:], True, 1)
    f3_low = send(va3[:, :CUT], True, 3)
    f3_high = send(vb3[:, CUT:], True, 1)
    own = [
        (s, [(0, 0) + full]),
        (t2, [(0, 1) + full, (0, 3) + full]),
        (o, [(0, 2) + full]),
        (va1, [(1, 0) + full]),
        (vb1, [(3, 0) + full]),
        (va2, [(1, 1) + full, (1, 3) + full]),
        (vb2, [(3, 1) + full, (3, 3) + full]),
        (va3, [(1, 2) + full]),
        (vb3, [(3, 2) + full]),
        (f1_low, [(2, 0) + low]),
        (f1_high, [(2, 0) + high]),
        (f2_a, [(2, 1) + full]),
        (f2_b, [(2, 3) + full]),
        (f3_low, [(2, 2) + low]),
        (f3_high, [(2, 2) + high]),
    ]
    pieces = []
    for x, places in own:
        pieces.append((x, [(0,) + p for p in places]))
        pieces.append((other_core(x), [(1,) + p for p in places]))
    return pieces


def assemble_kernel(places, *refs):
    n = len(places)
    sources, rows, tops, sem = refs[:n], refs[n], refs[n + 1], refs[n + 2]
    copies = []
    for ref, spots in zip(sources, places):
        for i, (core, v, u, first, count) in enumerate(spots):
            slot = core * 16 + v * 4 + u
            copies.append((ref.at[i], rows.at[pl.ds(slot * ROWS + first, count)]))
            if first + count == ROWS:
                copies.append((ref.at[i, count - 1], tops.at[slot]))
    started = []
    for k, (src, dst) in enumerate(copies):
        copy = pltpu.make_async_copy(src, dst, sem.at[k])
        copy.start()
        started.append(copy)
    for copy in started:
        copy.wait()


def assemble(pieces):
    arrays = [x for x, _ in pieces]
    places = [p for _, p in pieces]
    return pl.pallas_call(
        functools.partial(assemble_kernel, places),
        in_specs=[pl.BlockSpec(memory_space=pl.ANY)] * len(arrays),
        out_specs=[pl.BlockSpec(memory_space=pl.ANY)] * 2,
        out_shape=[
            jax.ShapeDtypeStruct((32 * ROWS, 16, 128), BF16),
            jax.ShapeDtypeStruct((32, 16, 128), BF16),
        ],
        scratch_shapes=[pltpu.SemaphoreType.DMA((96,))],
        name="assemble",
    )(*arrays)


def slots(owner, y, z, c):
    oy, oz, oc = owner // 8, owner // 2 % 4, owner % 2
    ry, rz = oy ^ y, oz ^ z
    return (oc ^ c) * 16 + jnp.where(oc == 0, rz * 4 + ry, ry * 4 + rz)


def picked(rows, gathered, base, entries):
    lane = lax.broadcasted_iota(jnp.int32, (16, 128), 1) < 64
    low, high = [], []
    for j in range(0, entries, 2):
        a, b = gathered[rows[base + j]], gathered[rows[base + j + 1]]
        low.append(jnp.where(lane, a, jnp.concatenate([b[:, 64:], b[:, :64]], axis=1)))
        high.append(jnp.where(lane, jnp.concatenate([a[:, 64:], a[:, :64]], axis=1), b))
    return jnp.concatenate([jnp.concatenate(low, axis=1), jnp.concatenate(high, axis=1)], axis=0)


def couple_kernel(leaf_rows, parent_rows, gathered, coupling, parent_coupling, leaf_far, parent_far):
    step = pl.program_id(0)
    for i in range(8):
        block = picked(leaf_rows, gathered, (step * 8 + i) * 16, 16)
        leaf_far[i] = dot(block, coupling[i].reshape(1024, 64))
    block = picked(parent_rows, gathered, step * 16, 16)
    parent_far[0] = dot(block, parent_coupling[0].reshape(1024, 64))


def couple(leaf_rows, parent_rows, gathered, coupling, parent_coupling):
    block = lambda *s: pl.BlockSpec(s, lambda i: (i,) + (0,) * (len(s) - 1))
    return pl.pallas_call(
        couple_kernel,
        grid=(8,),
        in_specs=[
            pl.BlockSpec(memory_space=pltpu.SMEM),
            pl.BlockSpec(memory_space=pltpu.SMEM),
            pl.BlockSpec(memory_space=pltpu.VMEM),
            block(8, 16, 64, 64),
            block(1, 16, 64, 64),
        ],
        out_specs=[block(8, 32, 64), block(1, 32, 64)],
        out_shape=[jax.ShapeDtypeStruct((64, 32, 64), F32), jax.ShapeDtypeStruct((8, 32, 64), F32)],
        compiler_params=pltpu.CompilerParams(vmem_limit_bytes=32 * MIB),
        cost_estimate=pl.CostEstimate(flops=2 * 72 * 32 * 64 * 1024, bytes_accessed=28 * MIB, transcendentals=0),
        name="couple",
    )(leaf_rows, parent_rows, gathered, coupling, parent_coupling)


def down_kernel(
    counts, top_rows, tops, top_coupling, parent_far, parent_descend, leaf_far, leaf_descend, out_basis, out, top_field
):
    step = pl.program_id(0)

    @pl.when(step == 0)
    def _():
        block = picked(top_rows, tops, 0, 16)
        top_field[...] = dot(block, top_coupling[0].reshape(1024, 64)).astype(BF16)

    parent = (parent_far[0] + dot(top_field[...], parent_descend[0])).astype(BF16)
    column = lax.broadcasted_iota(jnp.int32, (32, 256), 1)
    for i in range(8):
        field = (leaf_far[i] + dot(parent, leaf_descend[i])).astype(BF16)
        values = dot(field, out_basis[i])
        live = column < counts[step * 8 + i]
        out[i] = jnp.where(live, values, jnp.zeros_like(values)).astype(BF16)


def down(counts, top_rows, tops, top_coupling, parent_far, parent_descend, leaf_far, leaf_descend, out_basis):
    block = lambda *s: pl.BlockSpec(s, lambda i: (i,) + (0,) * (len(s) - 1))
    whole = pl.BlockSpec(memory_space=pltpu.VMEM)
    return pl.pallas_call(
        down_kernel,
        grid=(8,),
        in_specs=[
            pl.BlockSpec(memory_space=pltpu.SMEM),
            pl.BlockSpec(memory_space=pltpu.SMEM),
            whole,
            whole,
            block(1, 32, 64),
            block(1, 64, 64),
            block(8, 32, 64),
            block(8, 64, 64),
            block(8, 64, 256),
        ],
        out_specs=block(8, 32, 256),
        out_shape=jax.ShapeDtypeStruct((64, 32, 256), BF16),
        scratch_shapes=[pltpu.VMEM((32, 64), BF16)],
        compiler_params=pltpu.CompilerParams(vmem_limit_bytes=16 * MIB),
        cost_estimate=pl.CostEstimate(flops=2 * 64 * 32 * 64 * 320, bytes_accessed=6 * MIB, transcendentals=0),
        name="down",
    )(counts, top_rows, tops, top_coupling, parent_far, parent_descend, leaf_far, leaf_descend, out_basis)


def body(
    charges,
    counts,
    leaf_basis,
    out_basis,
    leaf_transfer,
    leaf_descend,
    parent_transfer,
    parent_descend,
    leaf_coupling,
    far_owner,
    far_local,
    parent_coupling,
    parent_owner,
    parent_index,
    top_coupling,
    top_source,
):
    x, y, z, c = (lax.axis_index(a) for a in "xyzc")
    leaf_rows = (slots(far_owner, y, z, c) * ROWS + far_local).reshape(-1)
    parent_rows = (slots(parent_owner, y, z, c) * ROWS + LEAF + parent_index).reshape(-1)
    top_rows = (((top_source // 32) ^ x) * 32 + slots(top_source % 32, y, z, c)).reshape(-1)

    coeffs = up(counts, charges, leaf_basis, leaf_transfer, parent_transfer)
    gathered, tops = assemble(gather_pieces(coeffs))
    planes = [tops] + [lax.ppermute(tops, "x", [(i, i ^ m) for i in range(4)]) for m in (1, 2, 3)]
    leaf_far, parent_far = couple(leaf_rows, parent_rows, gathered, leaf_coupling, parent_coupling)
    return down(
        counts,
        top_rows,
        jnp.concatenate(planes),
        top_coupling,
        parent_far,
        parent_descend,
        leaf_far,
        leaf_descend,
        out_basis,
    )


def solution(mesh):
    fine = Mesh(mesh.devices.reshape(4, 4, 4, 2), ("x", "y", "z", "c"))
    spec = P(("x", "y", "z", "c"))
    return jax.shard_map(body, mesh=fine, in_specs=(spec,) * 16, out_specs=spec, check_vma=False)
```

```python
import functools

import jax
import jax.numpy as jnp
from jax import lax
from jax.experimental import pallas as pl
from jax.experimental.pallas import tpu as pltpu
from jax.sharding import Mesh
from jax.sharding import PartitionSpec as P

BF16 = jnp.bfloat16
F32 = jnp.float32
LEAF, PARENT = 64, 8
ROWS = LEAF + PARENT + 1
NT = (((1,), (1,)), ((), ()))
MIB = 1 << 20


def dot(a, b):
    return jnp.dot(a, b, preferred_element_type=F32)


def pack(c):
    return jnp.concatenate([c[:16], c[16:]], axis=1)


def up_kernel(counts, charges, basis, transfer, parent_transfer, out, live, charge, base, move, lift, sem):
    chunks = 2
    size = LEAF // chunks
    count_copy = pltpu.make_async_copy(counts, live, sem.at[0])
    count_copy.start()
    copies = []
    for k in range(chunks):
        part = pl.ds(k * size, size)
        copies.append(
            [
                pltpu.make_async_copy(charges.at[part], charge.at[part], sem.at[3 + 2 * k]),
                pltpu.make_async_copy(basis.at[part], base.at[part], sem.at[4 + 2 * k]),
            ]
        )
        for copy in copies[k]:
            copy.start()
    transfers = [
        pltpu.make_async_copy(transfer, move, sem.at[1]),
        pltpu.make_async_copy(parent_transfer, lift, sem.at[2]),
    ]
    for copy in transfers:
        copy.start()
    count_copy.wait()
    column = lax.broadcasted_iota(jnp.int32, (32, 256), 1)
    coeffs = []
    for k in range(chunks):
        for copy in copies[k]:
            copy.wait()
        for b in range(k * size, (k + 1) * size):
            masked = jnp.where(column < live[b], charge[b], jnp.zeros((32, 256), BF16))
            coeff = lax.dot_general(masked, base[b], NT, preferred_element_type=F32).astype(BF16)
            out[b] = pack(coeff)
            coeffs.append(coeff)
    for copy in transfers:
        copy.wait()
    parents = []
    for q in range(PARENT):
        family = jnp.concatenate(coeffs[q * 8 : q * 8 + 8], axis=1)
        parents.append(dot(family, move[q * 8 : q * 8 + 8].reshape(512, 64)).astype(BF16))
        out[LEAF + q] = pack(parents[q])
    top = dot(jnp.concatenate(parents, axis=1), lift[...].reshape(512, 64))
    out[ROWS - 1] = pack(top.astype(BF16))


def up(*operands):
    hbm = pl.BlockSpec(memory_space=pltpu.HBM)
    return pl.pallas_call(
        up_kernel,
        in_specs=[hbm] * 5,
        out_specs=pl.BlockSpec(memory_space=pltpu.VMEM),
        out_shape=jax.ShapeDtypeStruct((ROWS, 16, 128), BF16),
        scratch_shapes=[pltpu.SMEM((LEAF,), jnp.int32)]
        + [pltpu.VMEM(x.shape, BF16) for x in operands[1:]]
        + [pltpu.SemaphoreType.DMA((7,))],
        compiler_params=pltpu.CompilerParams(vmem_limit_bytes=8 * MIB),
        cost_estimate=pl.CostEstimate(flops=2 * 64 * 32 * 64 * 320, bytes_accessed=5 * MIB, transcendentals=0),
        name="up",
    )(*operands)


def pairs(second, mask):
    out = []
    for y in range(4):
        for z in range(4):
            for c in range(2):
                along_y = (c == 0) != second
                ty, tz = (y ^ mask, z) if along_y else (y, z ^ mask)
                out.append(((y * 4 + z) * 2 + c, (ty * 4 + tz) * 2 + c))
    return out


def send(x, second, mask):
    return lax.ppermute(x, ("y", "z", "c"), pairs(second, mask))


def other_core(x):
    return lax.ppermute(x, "c", [(0, 1), (1, 0)])


def gather(s):
    s = s[None]
    a, o, b = (send(s, False, m) for m in (1, 2, 3))
    near, far = jnp.concatenate([s, a]), jnp.concatenate([o, b])
    near_a, near_b = send(near, True, 1), send(near, True, 3)
    far_a, far_b = send(far, True, 1), send(far, True, 3)
    near_o, far_o = send(near_a, True, 3), send(far_b, True, 1)
    early = [(near, 0), (far, 2), (near_a, 4), (far_a, 6), (near_b, 12), (far_b, 14)]
    return early, [(near_o, 8), (far_o, 10)]


def early_kernel(firsts, *refs):
    n = len(firsts)
    out, sem = refs[n:]
    copies = []
    for ref, first in zip(refs[:n], firsts):
        for i in range(2):
            spot = out.at[pl.ds((first + i) * ROWS, ROWS)]
            copies.append(pltpu.make_async_copy(ref.at[i], spot, sem.at[len(copies)]))
            copies[-1].start()
    for copy in copies:
        copy.wait()


def assemble_early(pieces):
    n = len(pieces)
    return pl.pallas_call(
        functools.partial(early_kernel, [first for _, first in pieces]),
        in_specs=[pl.BlockSpec(memory_space=pltpu.HBM)] * n,
        out_specs=pl.BlockSpec(memory_space=pltpu.VMEM),
        out_shape=jax.ShapeDtypeStruct((32 * ROWS, 16, 128), BF16),
        scratch_shapes=[pltpu.SemaphoreType.DMA((2 * n,))],
        compiler_params=pltpu.CompilerParams(vmem_limit_bytes=8 * MIB),
        cost_estimate=pl.CostEstimate(flops=0, bytes_accessed=4096, transcendentals=0),
        name="assemble_early",
    )(*[x for x, _ in pieces])


def late_kernel(firsts, *refs):
    out = refs[len(firsts) + 1]
    for ref, first in zip(refs, firsts):
        for i in range(2):
            out[(first + i) * ROWS : (first + i + 1) * ROWS] = ref[i]


def assemble_late(pieces, gathered):
    vmem = pl.BlockSpec(memory_space=pltpu.VMEM)
    n = len(pieces)
    return pl.pallas_call(
        functools.partial(late_kernel, [first for _, first in pieces]),
        in_specs=[vmem] * (n + 1),
        out_specs=vmem,
        out_shape=jax.ShapeDtypeStruct((32 * ROWS, 16, 128), BF16),
        input_output_aliases={n: 0},
        compiler_params=pltpu.CompilerParams(vmem_limit_bytes=8 * MIB),
        cost_estimate=pl.CostEstimate(flops=0, bytes_accessed=4096, transcendentals=0),
        name="assemble_late",
    )(*[x for x, _ in pieces], gathered)


def tops_kernel(firsts, *refs):
    n = len(firsts)
    out, sem = refs[n:]
    copies = []
    for ref, first in zip(refs[:n], firsts):
        for i in range(2):
            copies.append(pltpu.make_async_copy(ref.at[i, ROWS - 1], out.at[first + i], sem.at[len(copies)]))
            copies[-1].start()
    for copy in copies:
        copy.wait()


def column_tops(pieces):
    n = len(pieces)
    return pl.pallas_call(
        functools.partial(tops_kernel, [first for _, first in pieces]),
        in_specs=[pl.BlockSpec(memory_space=pltpu.HBM)] * n,
        out_specs=pl.BlockSpec(memory_space=pltpu.VMEM),
        out_shape=jax.ShapeDtypeStruct((16, 16, 128), BF16),
        scratch_shapes=[pltpu.SemaphoreType.DMA((2 * n,))],
        compiler_params=pltpu.CompilerParams(vmem_limit_bytes=4 * MIB),
        cost_estimate=pl.CostEstimate(flops=0, bytes_accessed=4096, transcendentals=0),
        name="tops",
    )(*[x for x, _ in pieces])


def slots(owner, y, z, c):
    oy, oz, oc = owner // 8, owner // 2 % 4, owner % 2
    ry, rz = oy ^ y, oz ^ z
    return (oc ^ c) * 16 + jnp.where(oc == 0, rz * 4 + ry, ry * 4 + rz)


def picked(load, entries):
    lane = lax.broadcasted_iota(jnp.int32, (16, 128), 1) < 64
    low, high = [], []
    for j in range(0, entries, 2):
        a, b = load(j), load(j + 1)
        low.append(jnp.where(lane, a, jnp.concatenate([b[:, 64:], b[:, :64]], axis=1)))
        high.append(jnp.where(lane, jnp.concatenate([a[:, 64:], a[:, :64]], axis=1), b))
    return jnp.concatenate([jnp.concatenate(low, axis=1), jnp.concatenate(high, axis=1)], axis=0)


def couple_kernel(
    place,
    far_owner,
    far_local,
    parent_owner,
    parent_index,
    gathered,
    coupling,
    parent_coupling,
    leaf_far,
    parent_far,
    leaf_rows,
    parent_rows,
    leaf_named,
    parent_named,
    sem,
):
    y, z, c = place[1], place[2], place[3]
    leaf_rows[...] = slots(far_owner[...], y, z, c) * ROWS + far_local[...]
    parent_rows[...] = slots(parent_owner[...], y, z, c) * ROWS + LEAF + parent_index[...]
    copies = [
        pltpu.make_async_copy(leaf_rows, leaf_named, sem.at[0]),
        pltpu.make_async_copy(parent_rows, parent_named, sem.at[1]),
    ]
    for copy in copies:
        copy.start()
    for copy in copies:
        copy.wait()

    def leaf(b, _):
        block = picked(lambda j: gathered[leaf_named[j, b]], 16)
        leaf_far[b] = dot(block, coupling[b].reshape(1024, 64))
        return 0

    def parent(q, _):
        block = picked(lambda j: gathered[parent_named[q, j]], 16)
        parent_far[q] = dot(block, parent_coupling[q].reshape(1024, 64))
        return 0

    lax.fori_loop(0, LEAF, leaf, 0, unroll=16)
    lax.fori_loop(0, PARENT, parent, 0, unroll=8)


def couple(place, far_owner, far_local, parent_owner, parent_index, gathered, coupling, parent_coupling):
    smem, vmem = pl.BlockSpec(memory_space=pltpu.SMEM), pl.BlockSpec(memory_space=pltpu.VMEM)
    return pl.pallas_call(
        couple_kernel,
        in_specs=[smem] + [vmem] * 7,
        out_specs=[vmem, vmem],
        out_shape=[jax.ShapeDtypeStruct((LEAF, 32, 64), F32), jax.ShapeDtypeStruct((PARENT, 32, 64), F32)],
        scratch_shapes=[
            pltpu.VMEM(far_owner.shape, jnp.int32),
            pltpu.VMEM(parent_owner.shape, jnp.int32),
            pltpu.SMEM(far_owner.shape, jnp.int32),
            pltpu.SMEM(parent_owner.shape, jnp.int32),
            pltpu.SemaphoreType.DMA((2,)),
        ],
        compiler_params=pltpu.CompilerParams(vmem_limit_bytes=4 * MIB),
        cost_estimate=pl.CostEstimate(flops=2 * 72 * 32 * 64 * 1024, bytes_accessed=28 * MIB, transcendentals=0),
        name="couple",
    )(place, far_owner, far_local, parent_owner, parent_index, gathered, coupling, parent_coupling)


def down_kernel(
    counts, place, top_source, tops, top_coupling, parent_far, parent_descend, leaf_far, leaf_descend, out_basis, out, values, sem
):
    x, y, z, c = (place[i] for i in range(4))

    def top(j):
        source = top_source[0, j]
        slot = slots(source % 32, y, z, c)
        return tops[slot // 16 * 64 + ((source // 32) ^ x) * 16 + slot % 16]

    block = picked(top, 16)
    top_field = dot(block, top_coupling[0].reshape(1024, 64)).astype(BF16)
    column = lax.broadcasted_iota(jnp.int32, (32, 256), 1)
    parents = [(parent_far[q] + dot(top_field, parent_descend[q])).astype(BF16) for q in range(PARENT)]
    copies = []
    for q in range(PARENT):
        for b in range(q * 8, q * 8 + 8):
            field = (leaf_far[b] + dot(parents[q], leaf_descend[b])).astype(BF16)
            value = dot(field, out_basis[b])
            values[b] = jnp.where(column < counts[b], value, jnp.zeros_like(value)).astype(BF16)
        part = pl.ds(q * 8, 8)
        copies.append(pltpu.make_async_copy(values.at[part], out.at[part], sem.at[q]))
        copies[q].start()
    for copy in copies:
        copy.wait()


def down(counts, place, top_source, *operands):
    smem, vmem = pl.BlockSpec(memory_space=pltpu.SMEM), pl.BlockSpec(memory_space=pltpu.VMEM)
    return pl.pallas_call(
        down_kernel,
        in_specs=[smem] * 3 + [vmem] * len(operands),
        out_specs=pl.BlockSpec(memory_space=pltpu.HBM),
        out_shape=jax.ShapeDtypeStruct((64, 32, 256), BF16),
        scratch_shapes=[pltpu.VMEM((64, 32, 256), BF16), pltpu.SemaphoreType.DMA((PARENT,))],
        compiler_params=pltpu.CompilerParams(vmem_limit_bytes=4 * MIB),
        cost_estimate=pl.CostEstimate(flops=2 * 64 * 32 * 64 * 320, bytes_accessed=6 * MIB, transcendentals=0),
        name="down",
    )(counts, place, top_source, *operands)


def body(
    charges,
    counts,
    leaf_basis,
    out_basis,
    leaf_transfer,
    leaf_descend,
    parent_transfer,
    parent_descend,
    leaf_coupling,
    far_owner,
    far_local,
    parent_coupling,
    parent_owner,
    parent_index,
    top_coupling,
    top_source,
):
    x, y, z, c = (lax.axis_index(a) for a in "xyzc")
    place = jnp.stack([x, y, z, c]).astype(jnp.int32)
    place, charges = lax.optimization_barrier((place, charges))

    hbm = lambda a: pltpu.with_memory_space_constraint(a, pltpu.HBM)
    coeffs = up(*map(hbm, (counts, charges, leaf_basis, leaf_transfer, parent_transfer)))
    early, late = gather(coeffs)
    swap = lambda pieces: [(other_core(piece), 16 + first) for piece, first in pieces]
    gathered = assemble_early(early + swap(early))
    gathered = assemble_late(late + swap(late), gathered)
    tops = column_tops(early + late)
    planes = [tops] + [lax.ppermute(tops, "x", [(i, i ^ m) for i in range(4)]) for m in (1, 2, 3)]

    names = (far_owner.T, far_local.T, parent_owner, parent_index)
    leaf_far, parent_far = couple(place, *names, gathered, leaf_coupling, parent_coupling)
    planes, leaf_far = lax.optimization_barrier((planes, leaf_far))
    tops = jnp.concatenate(planes)
    tops = jnp.concatenate([tops, other_core(tops)])
    return down(
        counts, place, top_source, tops, top_coupling, parent_far, parent_descend, leaf_far, leaf_descend, out_basis
    )


def solution(mesh):
    fine = Mesh(mesh.devices.reshape(4, 4, 4, 2), ("x", "y", "z", "c"))
    spec = P(("x", "y", "z", "c"))
    return jax.shard_map(body, mesh=fine, in_specs=(spec,) * 16, out_specs=spec, check_vma=False)
```

```python
import functools

import jax
import jax.numpy as jnp
from jax import lax
from jax.experimental import pallas as pl
from jax.experimental.pallas import tpu as pltpu
from jax.sharding import Mesh
from jax.sharding import PartitionSpec as P

BF16 = jnp.bfloat16
F32 = jnp.float32
LEAF, PARENT = 64, 8
ROWS = LEAF + PARENT + 1
NT = (((1,), (1,)), ((), ()))
MIB = 1 << 20


def dot(a, b):
    return jnp.dot(a, b, preferred_element_type=F32)


def pack(c):
    return jnp.concatenate([c[:16], c[16:]], axis=1)


def up_kernel(counts, charges, basis, transfer, parent_transfer, out, live, charge, base, move, lift, sem):
    chunks = 2
    size = LEAF // chunks
    count_copy = pltpu.make_async_copy(counts, live, sem.at[0])
    count_copy.start()
    copies = []
    for k in range(chunks):
        part = pl.ds(k * size, size)
        copies.append(
            [
                pltpu.make_async_copy(charges.at[part], charge.at[part], sem.at[3 + 2 * k]),
                pltpu.make_async_copy(basis.at[part], base.at[part], sem.at[4 + 2 * k]),
            ]
        )
        for copy in copies[k]:
            copy.start()
    transfers = [
        pltpu.make_async_copy(transfer, move, sem.at[1]),
        pltpu.make_async_copy(parent_transfer, lift, sem.at[2]),
    ]
    for copy in transfers:
        copy.start()
    count_copy.wait()
    column = lax.broadcasted_iota(jnp.int32, (32, 256), 1)
    coeffs = []
    for k in range(chunks):
        for copy in copies[k]:
            copy.wait()
        for b in range(k * size, (k + 1) * size):
            masked = jnp.where(column < live[b], charge[b], jnp.zeros((32, 256), BF16))
            coeff = lax.dot_general(masked, base[b], NT, preferred_element_type=F32).astype(BF16)
            out[b] = pack(coeff)
            coeffs.append(coeff)
    for copy in transfers:
        copy.wait()
    parents = []
    for q in range(PARENT):
        family = jnp.concatenate(coeffs[q * 8 : q * 8 + 8], axis=1)
        parents.append(dot(family, move[q * 8 : q * 8 + 8].reshape(512, 64)).astype(BF16))
        out[LEAF + q] = pack(parents[q])
    top = dot(jnp.concatenate(parents, axis=1), lift[...].reshape(512, 64))
    out[ROWS - 1] = pack(top.astype(BF16))


def up(*operands):
    hbm = pl.BlockSpec(memory_space=pltpu.HBM)
    return pl.pallas_call(
        up_kernel,
        in_specs=[hbm] * 5,
        out_specs=pl.BlockSpec(memory_space=pltpu.VMEM),
        out_shape=jax.ShapeDtypeStruct((ROWS, 16, 128), BF16),
        scratch_shapes=[pltpu.SMEM((LEAF,), jnp.int32)]
        + [pltpu.VMEM(x.shape, BF16) for x in operands[1:]]
        + [pltpu.SemaphoreType.DMA((7,))],
        compiler_params=pltpu.CompilerParams(vmem_limit_bytes=8 * MIB),
        cost_estimate=pl.CostEstimate(flops=2 * 64 * 32 * 64 * 320, bytes_accessed=5 * MIB, transcendentals=0),
        name="up",
    )(*operands)


def pairs(second, mask):
    out = []
    for y in range(4):
        for z in range(4):
            for c in range(2):
                along_y = (c == 0) != second
                ty, tz = (y ^ mask, z) if along_y else (y, z ^ mask)
                out.append(((y * 4 + z) * 2 + c, (ty * 4 + tz) * 2 + c))
    return out


def send(x, second, mask):
    return lax.ppermute(x, ("y", "z", "c"), pairs(second, mask))


def other_core(x):
    return lax.ppermute(x, "c", [(0, 1), (1, 0)])


def gather(s, staged):
    s = s[None]
    a, o, b = (send(s, False, m) for m in (1, 2, 3))
    near, far = jnp.concatenate([s, a]), jnp.concatenate([o, b])
    far, staged = lax.optimization_barrier((far, staged))
    near_a, near_b = send(near, True, 1), send(near, True, 3)
    far_a, far_b = send(far, True, 1), send(far, True, 3)
    near_o, far_o = send(near_a, True, 3), send(far_b, True, 1)
    early = [(near, 0), (far, 2), (near_a, 4), (far_a, 6), (near_b, 12), (far_b, 14)]
    return early, [(near_o, 8), (far_o, 10)], staged


def place_kernel(firsts, *refs):
    out = refs[-1]
    for ref, first in zip(refs, firsts):
        for i in range(2):
            out[(first + i) * ROWS : (first + i + 1) * ROWS] = ref[i]


def assemble(pieces, *earlier):
    vmem = pl.BlockSpec(memory_space=pltpu.VMEM)
    n = len(pieces)
    return pl.pallas_call(
        functools.partial(place_kernel, [first for _, first in pieces]),
        in_specs=[vmem] * (n + len(earlier)),
        out_specs=vmem,
        out_shape=jax.ShapeDtypeStruct((32 * ROWS, 16, 128), BF16),
        input_output_aliases={n: 0} if earlier else {},
        compiler_params=pltpu.CompilerParams(vmem_limit_bytes=10 * MIB),
        cost_estimate=pl.CostEstimate(flops=0, bytes_accessed=4096, transcendentals=0),
        name="assemble",
    )(*[x for x, _ in pieces], *earlier)


def tops_kernel(firsts, *refs):
    n = len(firsts)
    out, sem = refs[n:]
    copies = []
    for ref, first in zip(refs[:n], firsts):
        for i in range(2):
            copies.append(pltpu.make_async_copy(ref.at[i, ROWS - 1], out.at[first + i], sem.at[len(copies)]))
            copies[-1].start()
    for copy in copies:
        copy.wait()


def column_tops(pieces):
    n = len(pieces)
    return pl.pallas_call(
        functools.partial(tops_kernel, [first for _, first in pieces]),
        in_specs=[pl.BlockSpec(memory_space=pltpu.HBM)] * n,
        out_specs=pl.BlockSpec(memory_space=pltpu.VMEM),
        out_shape=jax.ShapeDtypeStruct((16, 16, 128), BF16),
        scratch_shapes=[pltpu.SemaphoreType.DMA((2 * n,))],
        compiler_params=pltpu.CompilerParams(vmem_limit_bytes=4 * MIB),
        cost_estimate=pl.CostEstimate(flops=0, bytes_accessed=4096, transcendentals=0),
        name="tops",
    )(*[x for x, _ in pieces])


def slots(owner, y, z, c):
    oy, oz, oc = owner // 8, owner // 2 % 4, owner % 2
    ry, rz = oy ^ y, oz ^ z
    return (oc ^ c) * 16 + jnp.where(oc == 0, rz * 4 + ry, ry * 4 + rz)


def picked(load, entries):
    lane = lax.broadcasted_iota(jnp.int32, (16, 128), 1) < 64
    low, high = [], []
    for j in range(0, entries, 2):
        a, b = load(j), load(j + 1)
        low.append(jnp.where(lane, a, jnp.concatenate([b[:, 64:], b[:, :64]], axis=1)))
        high.append(jnp.where(lane, jnp.concatenate([a[:, 64:], a[:, :64]], axis=1), b))
    return jnp.concatenate([jnp.concatenate(low, axis=1), jnp.concatenate(high, axis=1)], axis=0)


CHUNK = 8
STAGED = 24


def stage_kernel(coupling, out, sem):
    parts = 4
    size = out.shape[0] // parts
    copies = []
    for k in range(parts):
        source = coupling.at[pl.ds(k * size, size)]
        copies.append(pltpu.make_async_copy(source, out.at[pl.ds(k * size, size)], sem.at[k]))
        copies[k].start()
    for copy in copies:
        copy.wait()


def stage(coupling, count):
    return pl.pallas_call(
        stage_kernel,
        in_specs=[pl.BlockSpec(memory_space=pltpu.HBM)],
        out_specs=pl.BlockSpec(memory_space=pltpu.VMEM),
        out_shape=jax.ShapeDtypeStruct((count,) + coupling.shape[1:], BF16),
        scratch_shapes=[pltpu.SemaphoreType.DMA((4,))],
        compiler_params=pltpu.CompilerParams(vmem_limit_bytes=2 * MIB),
        cost_estimate=pl.CostEstimate(flops=0, bytes_accessed=4096, transcendentals=0),
        name="stage",
    )(pltpu.with_memory_space_constraint(coupling, pltpu.HBM))


def couple_kernel(
    place,
    far_owner,
    far_local,
    parent_owner,
    parent_index,
    gathered,
    head,
    coupling,
    parent_coupling,
    leaf_far,
    parent_far,
    staged,
    parent_staged,
    leaf_rows,
    parent_rows,
    leaf_named,
    parent_named,
    chunk_sem,
    row_sem,
):
    chunks = []
    for k in range((LEAF - STAGED) // CHUNK):
        source = coupling.at[pl.ds(STAGED + k * CHUNK, CHUNK)]
        chunks.append(pltpu.make_async_copy(source, staged.at[pl.ds(k * CHUNK, CHUNK)], chunk_sem.at[k]))
    chunks.append(pltpu.make_async_copy(parent_coupling, parent_staged, chunk_sem.at[len(chunks)]))
    for copy in chunks:
        copy.start()
    y, z, c = place[1], place[2], place[3]
    leaf_rows[...] = slots(far_owner[...], y, z, c) * ROWS + far_local[...]
    parent_rows[...] = slots(parent_owner[...], y, z, c) * ROWS + LEAF + parent_index[...]
    named = [
        pltpu.make_async_copy(leaf_rows, leaf_named, row_sem.at[0]),
        pltpu.make_async_copy(parent_rows, parent_named, row_sem.at[1]),
    ]
    for copy in named:
        copy.start()
    for copy in named:
        copy.wait()
    for b in range(STAGED):
        block = picked(lambda j: gathered[leaf_named[j, b]], 16)
        leaf_far[b] = dot(block, head[b].reshape(1024, 64))
    for k in range((LEAF - STAGED) // CHUNK):
        chunks[k].wait()
        for i in range(k * CHUNK, (k + 1) * CHUNK):
            block = picked(lambda j: gathered[leaf_named[j, STAGED + i]], 16)
            leaf_far[STAGED + i] = dot(block, staged[i].reshape(1024, 64))
    chunks[-1].wait()
    for q in range(PARENT):
        block = picked(lambda j: gathered[parent_named[q, j]], 16)
        parent_far[q] = dot(block, parent_staged[q].reshape(1024, 64))


def couple(place, far_owner, far_local, parent_owner, parent_index, gathered, head, coupling, parent_coupling):
    smem, vmem = pl.BlockSpec(memory_space=pltpu.SMEM), pl.BlockSpec(memory_space=pltpu.VMEM)
    return pl.pallas_call(
        couple_kernel,
        in_specs=[smem] + [vmem] * 6 + [pl.BlockSpec(memory_space=pltpu.HBM)] * 2,
        out_specs=[vmem, vmem],
        out_shape=[jax.ShapeDtypeStruct((LEAF, 32, 64), F32), jax.ShapeDtypeStruct((PARENT, 32, 64), F32)],
        scratch_shapes=[
            pltpu.VMEM((LEAF - STAGED,) + coupling.shape[1:], BF16),
            pltpu.VMEM(parent_coupling.shape, BF16),
            pltpu.VMEM(far_owner.shape, jnp.int32),
            pltpu.VMEM(parent_owner.shape, jnp.int32),
            pltpu.SMEM(far_owner.shape, jnp.int32),
            pltpu.SMEM(parent_owner.shape, jnp.int32),
            pltpu.SemaphoreType.DMA(((LEAF - STAGED) // CHUNK + 1,)),
            pltpu.SemaphoreType.DMA((2,)),
        ],
        compiler_params=pltpu.CompilerParams(vmem_limit_bytes=18 * MIB),
        cost_estimate=pl.CostEstimate(flops=2 * 72 * 32 * 64 * 1024, bytes_accessed=28 * MIB, transcendentals=0),
        name="couple",
    )(
        place,
        far_owner,
        far_local,
        parent_owner,
        parent_index,
        gathered,
        head,
        pltpu.with_memory_space_constraint(coupling, pltpu.HBM),
        pltpu.with_memory_space_constraint(parent_coupling, pltpu.HBM),
    )


def down_kernel(
    counts, place, top_source, tops, top_coupling, parent_far, parent_descend, leaf_far, leaf_descend, out_basis, out, values, sem
):
    x, y, z, c = (place[i] for i in range(4))

    def top(j):
        source = top_source[0, j]
        slot = slots(source % 32, y, z, c)
        return tops[slot // 16 * 64 + ((source // 32) ^ x) * 16 + slot % 16]

    block = picked(top, 16)
    top_field = dot(block, top_coupling[0].reshape(1024, 64)).astype(BF16)
    column = lax.broadcasted_iota(jnp.int32, (32, 256), 1)
    parents = [(parent_far[q] + dot(top_field, parent_descend[q])).astype(BF16) for q in range(PARENT)]
    copies = []
    for q in range(PARENT):
        for b in range(q * 8, q * 8 + 8):
            field = (leaf_far[b] + dot(parents[q], leaf_descend[b])).astype(BF16)
            value = dot(field, out_basis[b])
            values[b] = jnp.where(column < counts[b], value, jnp.zeros_like(value)).astype(BF16)
        part = pl.ds(q * 8, 8)
        copies.append(pltpu.make_async_copy(values.at[part], out.at[part], sem.at[q]))
        copies[q].start()
    for copy in copies:
        copy.wait()


def down(counts, place, top_source, *operands):
    smem, vmem = pl.BlockSpec(memory_space=pltpu.SMEM), pl.BlockSpec(memory_space=pltpu.VMEM)
    return pl.pallas_call(
        down_kernel,
        in_specs=[smem] * 3 + [vmem] * len(operands),
        out_specs=pl.BlockSpec(memory_space=pltpu.HBM),
        out_shape=jax.ShapeDtypeStruct((64, 32, 256), BF16),
        scratch_shapes=[pltpu.VMEM((64, 32, 256), BF16), pltpu.SemaphoreType.DMA((PARENT,))],
        compiler_params=pltpu.CompilerParams(vmem_limit_bytes=4 * MIB),
        cost_estimate=pl.CostEstimate(flops=2 * 64 * 32 * 64 * 320, bytes_accessed=6 * MIB, transcendentals=0),
        name="down",
    )(counts, place, top_source, *operands)


def body(
    charges,
    counts,
    leaf_basis,
    out_basis,
    leaf_transfer,
    leaf_descend,
    parent_transfer,
    parent_descend,
    leaf_coupling,
    far_owner,
    far_local,
    parent_coupling,
    parent_owner,
    parent_index,
    top_coupling,
    top_source,
):
    x, y, z, c = (lax.axis_index(a) for a in "xyzc")
    place = jnp.stack([x, y, z, c]).astype(jnp.int32)
    place, charges = lax.optimization_barrier((place, charges))

    hbm = lambda a: pltpu.with_memory_space_constraint(a, pltpu.HBM)
    coeffs = up(*map(hbm, (counts, charges, leaf_basis, leaf_transfer, parent_transfer)))
    early, late, head = gather(coeffs, stage(leaf_coupling, STAGED))
    swap = lambda pieces: [(other_core(piece), 16 + first) for piece, first in pieces]
    gathered = assemble(early + swap(early))
    gathered = assemble(late + swap(late), gathered)
    tops = column_tops(early + late)
    planes = [tops] + [lax.ppermute(tops, "x", [(i, i ^ m) for i in range(4)]) for m in (1, 2, 3)]

    names = (far_owner.T, far_local.T, parent_owner, parent_index)
    leaf_far, parent_far = couple(place, *names, gathered, head, leaf_coupling, parent_coupling)
    planes, leaf_far = lax.optimization_barrier((planes, leaf_far))
    tops = jnp.concatenate(planes)
    tops = jnp.concatenate([tops, other_core(tops)])
    return down(
        counts, place, top_source, tops, top_coupling, parent_far, parent_descend, leaf_far, leaf_descend, out_basis
    )


def solution(mesh):
    fine = Mesh(mesh.devices.reshape(4, 4, 4, 2), ("x", "y", "z", "c"))
    spec = P(("x", "y", "z", "c"))
    return jax.shard_map(body, mesh=fine, in_specs=(spec,) * 16, out_specs=spec, check_vma=False)
```

```python
import functools

import jax
import jax.numpy as jnp
from jax import lax
from jax.experimental import pallas as pl
from jax.experimental.pallas import tpu as pltpu
from jax.sharding import Mesh
from jax.sharding import PartitionSpec as P

BF16 = jnp.bfloat16
F32 = jnp.float32
LEAF, PARENT = 64, 8
ROWS = LEAF + PARENT + 1
NT = (((1,), (1,)), ((), ()))
MIB = 1 << 20


def dot(a, b):
    return jnp.dot(a, b, preferred_element_type=F32)


def pack(c):
    return jnp.concatenate([c[:16], c[16:]], axis=1)


def up_kernel(counts, charges, basis, transfer, parent_transfer, out, live, charge, base, move, lift, sem):
    chunks = 2
    size = LEAF // chunks
    count_copy = pltpu.make_async_copy(counts, live, sem.at[0])
    count_copy.start()
    copies = []
    for k in range(chunks):
        part = pl.ds(k * size, size)
        copies.append(
            [
                pltpu.make_async_copy(charges.at[part], charge.at[part], sem.at[3 + 2 * k]),
                pltpu.make_async_copy(basis.at[part], base.at[part], sem.at[4 + 2 * k]),
            ]
        )
        for copy in copies[k]:
            copy.start()
    transfers = [
        pltpu.make_async_copy(transfer, move, sem.at[1]),
        pltpu.make_async_copy(parent_transfer, lift, sem.at[2]),
    ]
    for copy in transfers:
        copy.start()
    count_copy.wait()
    column = lax.broadcasted_iota(jnp.int32, (32, 256), 1)
    coeffs = []
    for k in range(chunks):
        for copy in copies[k]:
            copy.wait()
        for b in range(k * size, (k + 1) * size):
            masked = jnp.where(column < live[b], charge[b], jnp.zeros((32, 256), BF16))
            coeff = lax.dot_general(masked, base[b], NT, preferred_element_type=F32).astype(BF16)
            out[b] = pack(coeff)
            coeffs.append(coeff)
    for copy in transfers:
        copy.wait()
    parents = []
    for q in range(PARENT):
        family = jnp.concatenate(coeffs[q * 8 : q * 8 + 8], axis=1)
        parents.append(dot(family, move[q * 8 : q * 8 + 8].reshape(512, 64)).astype(BF16))
        out[LEAF + q] = pack(parents[q])
    top = dot(jnp.concatenate(parents, axis=1), lift[...].reshape(512, 64))
    out[ROWS - 1] = pack(top.astype(BF16))


def up(*operands):
    hbm = pl.BlockSpec(memory_space=pltpu.HBM)
    return pl.pallas_call(
        up_kernel,
        in_specs=[hbm] * 5,
        out_specs=pl.BlockSpec(memory_space=pltpu.VMEM),
        out_shape=jax.ShapeDtypeStruct((ROWS, 16, 128), BF16),
        scratch_shapes=[pltpu.SMEM((LEAF,), jnp.int32)]
        + [pltpu.VMEM(x.shape, BF16) for x in operands[1:]]
        + [pltpu.SemaphoreType.DMA((7,))],
        compiler_params=pltpu.CompilerParams(vmem_limit_bytes=8 * MIB),
        cost_estimate=pl.CostEstimate(flops=2 * 64 * 32 * 64 * 320, bytes_accessed=5 * MIB, transcendentals=0),
        name="up",
    )(*operands)


def pairs(second, mask):
    out = []
    for y in range(4):
        for z in range(4):
            for c in range(2):
                along_y = (c == 0) != second
                ty, tz = (y ^ mask, z) if along_y else (y, z ^ mask)
                out.append(((y * 4 + z) * 2 + c, (ty * 4 + tz) * 2 + c))
    return out


def send(x, second, mask):
    return lax.ppermute(x, ("y", "z", "c"), pairs(second, mask))


def other_core(x):
    return lax.ppermute(x, "c", [(0, 1), (1, 0)])


def gather(s, staged):
    s = s[None]
    a, o, b = (send(s, False, m) for m in (1, 2, 3))
    near, far = jnp.concatenate([s, a]), jnp.concatenate([o, b])
    far, staged = lax.optimization_barrier((far, staged))
    near_a, near_b = send(near, True, 1), send(near, True, 3)
    far_a, far_b = send(far, True, 1), send(far, True, 3)
    near_o, far_o = send(near_a, True, 3), send(far_b, True, 1)
    early = [(near, 0), (far, 2), (near_a, 4), (far_a, 6), (near_b, 12), (far_b, 14)]
    return early, [(near_o, 8), (far_o, 10)], staged


def place_kernel(firsts, *refs):
    out = refs[-1]
    for ref, first in zip(refs, firsts):
        for i in range(2):
            out[(first + i) * ROWS : (first + i + 1) * ROWS] = ref[i]


def assemble(pieces, *earlier):
    vmem = pl.BlockSpec(memory_space=pltpu.VMEM)
    n = len(pieces)
    return pl.pallas_call(
        functools.partial(place_kernel, [first for _, first in pieces]),
        in_specs=[vmem] * (n + len(earlier)),
        out_specs=vmem,
        out_shape=jax.ShapeDtypeStruct((32 * ROWS, 16, 128), BF16),
        input_output_aliases={n: 0} if earlier else {},
        compiler_params=pltpu.CompilerParams(vmem_limit_bytes=10 * MIB),
        cost_estimate=pl.CostEstimate(flops=0, bytes_accessed=4096, transcendentals=0),
        name="assemble",
    )(*[x for x, _ in pieces], *earlier)


def tops_kernel(firsts, *refs):
    n = len(firsts)
    out, sem = refs[n:]
    copies = []
    for ref, first in zip(refs[:n], firsts):
        for i in range(2):
            copies.append(pltpu.make_async_copy(ref.at[i, ROWS - 1], out.at[first + i], sem.at[len(copies)]))
            copies[-1].start()
    for copy in copies:
        copy.wait()


def column_tops(pieces):
    n = len(pieces)
    return pl.pallas_call(
        functools.partial(tops_kernel, [first for _, first in pieces]),
        in_specs=[pl.BlockSpec(memory_space=pltpu.HBM)] * n,
        out_specs=pl.BlockSpec(memory_space=pltpu.VMEM),
        out_shape=jax.ShapeDtypeStruct((16, 16, 128), BF16),
        scratch_shapes=[pltpu.SemaphoreType.DMA((2 * n,))],
        compiler_params=pltpu.CompilerParams(vmem_limit_bytes=4 * MIB),
        cost_estimate=pl.CostEstimate(flops=0, bytes_accessed=4096, transcendentals=0),
        name="tops",
    )(*[x for x, _ in pieces])


def slots(owner, y, z, c):
    oy, oz, oc = owner // 8, owner // 2 % 4, owner % 2
    ry, rz = oy ^ y, oz ^ z
    return (oc ^ c) * 16 + jnp.where(oc == 0, rz * 4 + ry, ry * 4 + rz)


def picked(load, entries):
    lane = lax.broadcasted_iota(jnp.int32, (16, 128), 1) < 64
    low, high = [], []
    for j in range(0, entries, 2):
        a, b = load(j), load(j + 1)
        low.append(jnp.where(lane, a, jnp.concatenate([b[:, 64:], b[:, :64]], axis=1)))
        high.append(jnp.where(lane, jnp.concatenate([a[:, 64:], a[:, :64]], axis=1), b))
    return jnp.concatenate([jnp.concatenate(low, axis=1), jnp.concatenate(high, axis=1)], axis=0)


CHUNK = 8
STAGED = 16


def stage_kernel(place, *refs):
    names, coupling, head, leaf_rows, parent_rows, top_rows = refs[:5], refs[5], *refs[6:10]
    held, sem = refs[10:15], refs[15]
    reads = [pltpu.make_async_copy(src, dst, sem.at[i]) for i, (src, dst) in enumerate(zip(names, held))]
    parts = 4
    size = head.shape[0] // parts
    copies = []
    for k in range(parts):
        part = pl.ds(k * size, size)
        copies.append(pltpu.make_async_copy(coupling.at[part], head.at[part], sem.at[5 + k]))
    for copy in reads + copies:
        copy.start()
    for copy in reads:
        copy.wait()
    x, y, z, c = (place[i] for i in range(4))
    far_owner, far_local, parent_owner, parent_index, source = (ref[...] for ref in held)
    leaf_rows[...] = slots(far_owner, y, z, c) * ROWS + far_local
    parent_rows[...] = slots(parent_owner, y, z, c) * ROWS + LEAF + parent_index
    slot = slots(source % 32, y, z, c)
    top_rows[...] = slot // 16 * 64 + ((source // 32) ^ x) * 16 + slot % 16
    for copy in copies:
        copy.wait()


def stage(place, far_owner, far_local, parent_owner, parent_index, top_source, coupling, count):
    smem, vmem = pl.BlockSpec(memory_space=pltpu.SMEM), pl.BlockSpec(memory_space=pltpu.VMEM)
    names = (far_owner, far_local, parent_owner, parent_index, top_source)
    hbm = lambda a: pltpu.with_memory_space_constraint(a, pltpu.HBM)
    return pl.pallas_call(
        stage_kernel,
        in_specs=[smem] + [pl.BlockSpec(memory_space=pltpu.HBM)] * 6,
        out_specs=[vmem] * 4,
        out_shape=[jax.ShapeDtypeStruct((count,) + coupling.shape[1:], BF16)]
        + [jax.ShapeDtypeStruct(x.shape, jnp.int32) for x in (far_owner, parent_owner, top_source)],
        scratch_shapes=[pltpu.VMEM(x.shape, jnp.int32) for x in names] + [pltpu.SemaphoreType.DMA((9,))],
        compiler_params=pltpu.CompilerParams(vmem_limit_bytes=2 * MIB),
        cost_estimate=pl.CostEstimate(flops=0, bytes_accessed=4096, transcendentals=0),
        name="stage",
    )(place, *map(hbm, names), hbm(coupling))


def couple_kernel(
    leaf_rows, gathered, head, coupling, parent_coupling, leaf_far, parent_staged, staged, leaf_named, chunk_sem, row_sem
):
    chunks = []
    for k in range((LEAF - STAGED) // CHUNK):
        source = coupling.at[pl.ds(STAGED + k * CHUNK, CHUNK)]
        chunks.append(pltpu.make_async_copy(source, staged.at[pl.ds(k * CHUNK, CHUNK)], chunk_sem.at[k]))
    chunks.append(pltpu.make_async_copy(parent_coupling, parent_staged, chunk_sem.at[len(chunks)]))
    named = pltpu.make_async_copy(leaf_rows, leaf_named, row_sem)
    for copy in [named] + chunks:
        copy.start()
    named.wait()
    for b in range(STAGED):
        block = picked(lambda j: gathered[leaf_named[j, b]], 16)
        leaf_far[b] = dot(block, head[b].reshape(1024, 64))
    for k in range((LEAF - STAGED) // CHUNK):
        chunks[k].wait()
        for i in range(k * CHUNK, (k + 1) * CHUNK):
            block = picked(lambda j: gathered[leaf_named[j, STAGED + i]], 16)
            leaf_far[STAGED + i] = dot(block, staged[i].reshape(1024, 64))
    chunks[-1].wait()


def couple_parents_kernel(parent_rows, gathered, coupling, far, named, sem):
    copy = pltpu.make_async_copy(parent_rows, named, sem)
    copy.start()
    copy.wait()
    for q in range(PARENT):
        block = picked(lambda j: gathered[named[q, j]], 16)
        far[q] = dot(block, coupling[q].reshape(1024, 64))


def couple_parents(parent_rows, gathered, coupling):
    vmem = pl.BlockSpec(memory_space=pltpu.VMEM)
    return pl.pallas_call(
        couple_parents_kernel,
        in_specs=[vmem] * 3,
        out_specs=vmem,
        out_shape=jax.ShapeDtypeStruct((PARENT, 32, 64), F32),
        scratch_shapes=[pltpu.SMEM(parent_rows.shape, jnp.int32), pltpu.SemaphoreType.DMA],
        compiler_params=pltpu.CompilerParams(vmem_limit_bytes=4 * MIB),
        cost_estimate=pl.CostEstimate(flops=2 * 8 * 32 * 64 * 1024, bytes_accessed=3 * MIB, transcendentals=0),
        name="couple_parents",
    )(parent_rows, gathered, coupling)


def couple(leaf_rows, gathered, head, coupling, parent_coupling):
    vmem = pl.BlockSpec(memory_space=pltpu.VMEM)
    return pl.pallas_call(
        couple_kernel,
        in_specs=[vmem] * 3 + [pl.BlockSpec(memory_space=pltpu.HBM)] * 2,
        out_specs=[vmem, vmem],
        out_shape=[jax.ShapeDtypeStruct((LEAF, 32, 64), F32), jax.ShapeDtypeStruct(parent_coupling.shape, BF16)],
        scratch_shapes=[
            pltpu.VMEM((LEAF - STAGED,) + coupling.shape[1:], BF16),
            pltpu.SMEM(leaf_rows.shape, jnp.int32),
            pltpu.SemaphoreType.DMA(((LEAF - STAGED) // CHUNK + 1,)),
            pltpu.SemaphoreType.DMA,
        ],
        compiler_params=pltpu.CompilerParams(vmem_limit_bytes=18 * MIB),
        cost_estimate=pl.CostEstimate(flops=2 * 72 * 32 * 64 * 1024, bytes_accessed=28 * MIB, transcendentals=0),
        name="couple",
    )(
        leaf_rows,
        gathered,
        head,
        pltpu.with_memory_space_constraint(coupling, pltpu.HBM),
        pltpu.with_memory_space_constraint(parent_coupling, pltpu.HBM),
    )


def down_kernel(
    counts, top_rows, tops, top_coupling, parent_far, parent_descend, leaf_far, leaf_descend, out_basis, out, values, sem
):
    block = picked(lambda j: tops[top_rows[0, j]], 16)
    top_field = dot(block, top_coupling[0].reshape(1024, 64)).astype(BF16)
    column = lax.broadcasted_iota(jnp.int32, (32, 256), 1)
    parents = [(parent_far[q] + dot(top_field, parent_descend[q])).astype(BF16) for q in range(PARENT)]
    copies = []
    for q in range(PARENT):
        for b in range(q * 8, q * 8 + 8):
            field = (leaf_far[b] + dot(parents[q], leaf_descend[b])).astype(BF16)
            value = dot(field, out_basis[b])
            values[b] = jnp.where(column < counts[b], value, jnp.zeros_like(value)).astype(BF16)
        part = pl.ds(q * 8, 8)
        copies.append(pltpu.make_async_copy(values.at[part], out.at[part], sem.at[q]))
        copies[q].start()
    for copy in copies:
        copy.wait()


def down(counts, top_rows, *operands):
    smem, vmem = pl.BlockSpec(memory_space=pltpu.SMEM), pl.BlockSpec(memory_space=pltpu.VMEM)
    return pl.pallas_call(
        down_kernel,
        in_specs=[smem] * 2 + [vmem] * len(operands),
        out_specs=pl.BlockSpec(memory_space=pltpu.HBM),
        out_shape=jax.ShapeDtypeStruct((64, 32, 256), BF16),
        scratch_shapes=[pltpu.VMEM((64, 32, 256), BF16), pltpu.SemaphoreType.DMA((PARENT,))],
        compiler_params=pltpu.CompilerParams(vmem_limit_bytes=4 * MIB),
        cost_estimate=pl.CostEstimate(flops=2 * 64 * 32 * 64 * 320, bytes_accessed=6 * MIB, transcendentals=0),
        name="down",
    )(counts, top_rows, *operands)


def body(
    charges,
    counts,
    leaf_basis,
    out_basis,
    leaf_transfer,
    leaf_descend,
    parent_transfer,
    parent_descend,
    leaf_coupling,
    far_owner,
    far_local,
    parent_coupling,
    parent_owner,
    parent_index,
    top_coupling,
    top_source,
):
    x, y, z, c = (lax.axis_index(a) for a in "xyzc")
    place = jnp.stack([x, y, z, c]).astype(jnp.int32)
    place, charges = lax.optimization_barrier((place, charges))

    hbm = lambda a: pltpu.with_memory_space_constraint(a, pltpu.HBM)
    coeffs = up(*map(hbm, (counts, charges, leaf_basis, leaf_transfer, parent_transfer)))
    names = (far_owner.T, far_local.T, parent_owner, parent_index, top_source)
    early, late, prepared = gather(coeffs, stage(place, *names, leaf_coupling, STAGED))
    head, leaf_rows, parent_rows, top_rows = prepared
    swap = lambda pieces: [(other_core(piece), 16 + first) for piece, first in pieces]
    gathered = assemble(early + swap(early))
    gathered = assemble(late + swap(late), gathered)
    tops = column_tops(early + late)
    planes = [tops] + [lax.ppermute(tops, "x", [(i, i ^ m) for i in range(4)]) for m in (1, 2, 3)]

    leaf_far, parent_staged = couple(leaf_rows, gathered, head, leaf_coupling, parent_coupling)
    planes, leaf_far = lax.optimization_barrier((planes, leaf_far))
    tops = jnp.concatenate(planes)
    tops = jnp.concatenate([tops, other_core(tops)])
    parent_far = couple_parents(parent_rows, gathered, parent_staged)
    return down(
        counts, top_rows, tops, top_coupling, parent_far, parent_descend, leaf_far, leaf_descend, out_basis
    )


def solution(mesh):
    fine = Mesh(mesh.devices.reshape(4, 4, 4, 2), ("x", "y", "z", "c"))
    spec = P(("x", "y", "z", "c"))
    return jax.shard_map(body, mesh=fine, in_specs=(spec,) * 16, out_specs=spec, check_vma=False)
```

```python
import functools

import jax
import jax.numpy as jnp
from jax import lax
from jax.experimental import pallas as pl
from jax.experimental.pallas import tpu as pltpu
from jax.sharding import Mesh
from jax.sharding import PartitionSpec as P

BF16 = jnp.bfloat16
F32 = jnp.float32
LEAF, PARENT = 64, 8
ROWS = LEAF + PARENT + 1
MORE = 16
NT = (((1,), (1,)), ((), ()))
MIB = 1 << 20


def dot(a, b):
    return jnp.dot(a, b, preferred_element_type=F32)


def pack(c):
    return jnp.concatenate([c[:16], c[16:]], axis=1)


def up_kernel(counts, charges, basis, transfer, parent_transfer, out, live, charge, base, move, lift, sem):
    chunks = 2
    size = LEAF // chunks
    count_copy = pltpu.make_async_copy(counts, live, sem.at[0])
    count_copy.start()
    copies = []
    for k in range(chunks):
        part = pl.ds(k * size, size)
        copies.append(
            [
                pltpu.make_async_copy(charges.at[part], charge.at[part], sem.at[3 + 2 * k]),
                pltpu.make_async_copy(basis.at[part], base.at[part], sem.at[4 + 2 * k]),
            ]
        )
        for copy in copies[k]:
            copy.start()
    transfers = [
        pltpu.make_async_copy(transfer, move, sem.at[1]),
        pltpu.make_async_copy(parent_transfer, lift, sem.at[2]),
    ]
    for copy in transfers:
        copy.start()
    count_copy.wait()
    column = lax.broadcasted_iota(jnp.int32, (32, 256), 1)
    coeffs = []
    for k in range(chunks):
        for copy in copies[k]:
            copy.wait()
        for b in range(k * size, (k + 1) * size):
            masked = jnp.where(column < live[b], charge[b], jnp.zeros((32, 256), BF16))
            coeff = lax.dot_general(masked, base[b], NT, preferred_element_type=F32).astype(BF16)
            out[b] = pack(coeff)
            coeffs.append(coeff)
    for copy in transfers:
        copy.wait()
    parents = []
    for q in range(PARENT):
        family = jnp.concatenate(coeffs[q * 8 : q * 8 + 8], axis=1)
        parents.append(dot(family, move[q * 8 : q * 8 + 8].reshape(512, 64)).astype(BF16))
        out[LEAF + q] = pack(parents[q])
    top = dot(jnp.concatenate(parents, axis=1), lift[...].reshape(512, 64))
    out[ROWS - 1] = pack(top.astype(BF16))


def up(*operands):
    hbm = pl.BlockSpec(memory_space=pltpu.HBM)
    return pl.pallas_call(
        up_kernel,
        in_specs=[hbm] * 5,
        out_specs=pl.BlockSpec(memory_space=pltpu.VMEM),
        out_shape=jax.ShapeDtypeStruct((ROWS, 16, 128), BF16),
        scratch_shapes=[pltpu.SMEM((LEAF,), jnp.int32)]
        + [pltpu.VMEM(x.shape, BF16) for x in operands[1:]]
        + [pltpu.SemaphoreType.DMA((7,))],
        compiler_params=pltpu.CompilerParams(vmem_limit_bytes=8 * MIB),
        cost_estimate=pl.CostEstimate(flops=2 * 64 * 32 * 64 * 320, bytes_accessed=5 * MIB, transcendentals=0),
        name="up",
    )(*operands)


def pairs(second, mask):
    out = []
    for y in range(4):
        for z in range(4):
            for c in range(2):
                along_y = (c == 0) != second
                ty, tz = (y ^ mask, z) if along_y else (y, z ^ mask)
                out.append(((y * 4 + z) * 2 + c, (ty * 4 + tz) * 2 + c))
    return out


def send(x, second, mask):
    return lax.ppermute(x, ("y", "z", "c"), pairs(second, mask))


def other_core(x):
    return lax.ppermute(x, "c", [(0, 1), (1, 0)])


def gather(s, staged, more):
    s = s[None]
    a, o, b = (send(s, False, m) for m in (1, 2, 3))
    near, far = jnp.concatenate([s, a]), jnp.concatenate([o, b])
    far, staged = lax.optimization_barrier((far, staged))
    near_a, near_b = send(near, True, 1), send(near, True, 3)
    far_a, far_b = send(far, True, 1), send(far, True, 3)
    near_b, more = lax.optimization_barrier((near_b, more))
    near_o, far_o = send(near_a, True, 3), send(far_b, True, 1)
    early = [(near, 0), (far, 2), (near_a, 4), (far_a, 6), (near_b, 12), (far_b, 14)]
    return early, [(near_o, 8), (far_o, 10)], staged, more


def place_kernel(firsts, *refs):
    out = refs[-1]
    for ref, first in zip(refs, firsts):
        for i in range(2):
            out[(first + i) * ROWS : (first + i + 1) * ROWS] = ref[i]


def assemble(pieces, *earlier):
    vmem = pl.BlockSpec(memory_space=pltpu.VMEM)
    n = len(pieces)
    return pl.pallas_call(
        functools.partial(place_kernel, [first for _, first in pieces]),
        in_specs=[vmem] * (n + len(earlier)),
        out_specs=vmem,
        out_shape=jax.ShapeDtypeStruct((32 * ROWS, 16, 128), BF16),
        input_output_aliases={n: 0} if earlier else {},
        compiler_params=pltpu.CompilerParams(vmem_limit_bytes=10 * MIB),
        cost_estimate=pl.CostEstimate(flops=0, bytes_accessed=4096, transcendentals=0),
        name="assemble",
    )(*[x for x, _ in pieces], *earlier)


def tops_kernel(firsts, *refs):
    n = len(firsts)
    out, sem = refs[n:]
    copies = []
    for ref, first in zip(refs[:n], firsts):
        for i in range(2):
            copies.append(pltpu.make_async_copy(ref.at[i, ROWS - 1], out.at[first + i], sem.at[len(copies)]))
            copies[-1].start()
    for copy in copies:
        copy.wait()


def column_tops(pieces):
    n = len(pieces)
    return pl.pallas_call(
        functools.partial(tops_kernel, [first for _, first in pieces]),
        in_specs=[pl.BlockSpec(memory_space=pltpu.HBM)] * n,
        out_specs=pl.BlockSpec(memory_space=pltpu.VMEM),
        out_shape=jax.ShapeDtypeStruct((16, 16, 128), BF16),
        scratch_shapes=[pltpu.SemaphoreType.DMA((2 * n,))],
        compiler_params=pltpu.CompilerParams(vmem_limit_bytes=4 * MIB),
        cost_estimate=pl.CostEstimate(flops=0, bytes_accessed=4096, transcendentals=0),
        name="tops",
    )(*[x for x, _ in pieces])


def slots(owner, y, z, c):
    oy, oz, oc = owner // 8, owner // 2 % 4, owner % 2
    ry, rz = oy ^ y, oz ^ z
    return (oc ^ c) * 16 + jnp.where(oc == 0, rz * 4 + ry, ry * 4 + rz)


def picked(load, entries):
    lane = lax.broadcasted_iota(jnp.int32, (16, 128), 1) < 64
    low, high = [], []
    for j in range(0, entries, 2):
        a, b = load(j), load(j + 1)
        low.append(jnp.where(lane, a, jnp.concatenate([b[:, 64:], b[:, :64]], axis=1)))
        high.append(jnp.where(lane, jnp.concatenate([a[:, 64:], a[:, :64]], axis=1), b))
    return jnp.concatenate([jnp.concatenate(low, axis=1), jnp.concatenate(high, axis=1)], axis=0)


CHUNK = 8
STAGED = 16


def stage_kernel(place, *refs):
    names, coupling, head, leaf_rows, parent_rows, top_rows = refs[:5], refs[5], *refs[6:10]
    held, sem = refs[10:15], refs[15]
    reads = [pltpu.make_async_copy(src, dst, sem.at[i]) for i, (src, dst) in enumerate(zip(names, held))]
    parts = 4
    size = head.shape[0] // parts
    copies = []
    for k in range(parts):
        part = pl.ds(k * size, size)
        copies.append(pltpu.make_async_copy(coupling.at[part], head.at[part], sem.at[5 + k]))
    for copy in reads + copies:
        copy.start()
    for copy in reads:
        copy.wait()
    x, y, z, c = (place[i] for i in range(4))
    far_owner, far_local, parent_owner, parent_index, source = (ref[...] for ref in held)
    leaf_rows[...] = slots(far_owner, y, z, c) * ROWS + far_local
    parent_rows[...] = slots(parent_owner, y, z, c) * ROWS + LEAF + parent_index
    slot = slots(source % 32, y, z, c)
    top_rows[...] = slot // 16 * 64 + ((source // 32) ^ x) * 16 + slot % 16
    for copy in copies:
        copy.wait()


def stage(place, far_owner, far_local, parent_owner, parent_index, top_source, coupling, count):
    smem, vmem = pl.BlockSpec(memory_space=pltpu.SMEM), pl.BlockSpec(memory_space=pltpu.VMEM)
    names = (far_owner, far_local, parent_owner, parent_index, top_source)
    hbm = lambda a: pltpu.with_memory_space_constraint(a, pltpu.HBM)
    return pl.pallas_call(
        stage_kernel,
        in_specs=[smem] + [pl.BlockSpec(memory_space=pltpu.HBM)] * 6,
        out_specs=[vmem] * 4,
        out_shape=[jax.ShapeDtypeStruct((count,) + coupling.shape[1:], BF16)]
        + [jax.ShapeDtypeStruct(x.shape, jnp.int32) for x in (far_owner, parent_owner, top_source)],
        scratch_shapes=[pltpu.VMEM(x.shape, jnp.int32) for x in names] + [pltpu.SemaphoreType.DMA((9,))],
        compiler_params=pltpu.CompilerParams(vmem_limit_bytes=2 * MIB),
        cost_estimate=pl.CostEstimate(flops=0, bytes_accessed=4096, transcendentals=0),
        name="stage",
    )(place, *map(hbm, names), hbm(coupling))


def stage_more_kernel(coupling, out, sem):
    parts = 4
    size = out.shape[0] // parts
    copies = []
    for k in range(parts):
        source = coupling.at[pl.ds(STAGED + k * size, size)]
        copies.append(pltpu.make_async_copy(source, out.at[pl.ds(k * size, size)], sem.at[k]))
        copies[k].start()
    for copy in copies:
        copy.wait()


def stage_more(coupling):
    return pl.pallas_call(
        stage_more_kernel,
        in_specs=[pl.BlockSpec(memory_space=pltpu.HBM)],
        out_specs=pl.BlockSpec(memory_space=pltpu.VMEM),
        out_shape=jax.ShapeDtypeStruct((MORE,) + coupling.shape[1:], BF16),
        scratch_shapes=[pltpu.SemaphoreType.DMA((4,))],
        compiler_params=pltpu.CompilerParams(vmem_limit_bytes=2 * MIB),
        cost_estimate=pl.CostEstimate(flops=0, bytes_accessed=4096, transcendentals=0),
        name="stage_more",
    )(pltpu.with_memory_space_constraint(coupling, pltpu.HBM))


def couple_kernel(
    leaf_rows, gathered, head, more, coupling, parent_coupling, leaf_far, parent_staged, staged, leaf_named, chunk_sem, row_sem
):
    chunks = []
    for k in range((LEAF - STAGED - MORE) // CHUNK):
        source = coupling.at[pl.ds(STAGED + MORE + k * CHUNK, CHUNK)]
        chunks.append(pltpu.make_async_copy(source, staged.at[pl.ds(k * CHUNK, CHUNK)], chunk_sem.at[k]))
    chunks.append(pltpu.make_async_copy(parent_coupling, parent_staged, chunk_sem.at[len(chunks)]))
    named = pltpu.make_async_copy(leaf_rows, leaf_named, row_sem)
    for copy in [named] + chunks:
        copy.start()
    named.wait()
    for b in range(STAGED):
        block = picked(lambda j: gathered[leaf_named[j, b]], 16)
        leaf_far[b] = dot(block, head[b].reshape(1024, 64))
    for i in range(MORE):
        block = picked(lambda j: gathered[leaf_named[j, STAGED + i]], 16)
        leaf_far[STAGED + i] = dot(block, more[i].reshape(1024, 64))
    for k in range((LEAF - STAGED - MORE) // CHUNK):
        chunks[k].wait()
        for i in range(k * CHUNK, (k + 1) * CHUNK):
            block = picked(lambda j: gathered[leaf_named[j, STAGED + MORE + i]], 16)
            leaf_far[STAGED + MORE + i] = dot(block, staged[i].reshape(1024, 64))
    chunks[-1].wait()


def couple_parents_kernel(parent_rows, gathered, coupling, far, named, sem):
    copy = pltpu.make_async_copy(parent_rows, named, sem)
    copy.start()
    copy.wait()
    for q in range(PARENT):
        block = picked(lambda j: gathered[named[q, j]], 16)
        far[q] = dot(block, coupling[q].reshape(1024, 64))


def couple_parents(parent_rows, gathered, coupling):
    vmem = pl.BlockSpec(memory_space=pltpu.VMEM)
    return pl.pallas_call(
        couple_parents_kernel,
        in_specs=[vmem] * 3,
        out_specs=vmem,
        out_shape=jax.ShapeDtypeStruct((PARENT, 32, 64), F32),
        scratch_shapes=[pltpu.SMEM(parent_rows.shape, jnp.int32), pltpu.SemaphoreType.DMA],
        compiler_params=pltpu.CompilerParams(vmem_limit_bytes=4 * MIB),
        cost_estimate=pl.CostEstimate(flops=2 * 8 * 32 * 64 * 1024, bytes_accessed=3 * MIB, transcendentals=0),
        name="couple_parents",
    )(parent_rows, gathered, coupling)


def couple(leaf_rows, gathered, head, more, coupling, parent_coupling):
    vmem = pl.BlockSpec(memory_space=pltpu.VMEM)
    return pl.pallas_call(
        couple_kernel,
        in_specs=[vmem] * 4 + [pl.BlockSpec(memory_space=pltpu.HBM)] * 2,
        out_specs=[vmem, vmem],
        out_shape=[jax.ShapeDtypeStruct((LEAF, 32, 64), F32), jax.ShapeDtypeStruct(parent_coupling.shape, BF16)],
        scratch_shapes=[
            pltpu.VMEM((LEAF - STAGED - MORE,) + coupling.shape[1:], BF16),
            pltpu.SMEM(leaf_rows.shape, jnp.int32),
            pltpu.SemaphoreType.DMA(((LEAF - STAGED - MORE) // CHUNK + 1,)),
            pltpu.SemaphoreType.DMA,
        ],
        compiler_params=pltpu.CompilerParams(vmem_limit_bytes=18 * MIB),
        cost_estimate=pl.CostEstimate(flops=2 * 72 * 32 * 64 * 1024, bytes_accessed=28 * MIB, transcendentals=0),
        name="couple",
    )(
        leaf_rows,
        gathered,
        head,
        more,
        pltpu.with_memory_space_constraint(coupling, pltpu.HBM),
        pltpu.with_memory_space_constraint(parent_coupling, pltpu.HBM),
    )


def down_kernel(
    counts, top_rows, tops, top_coupling, parent_far, parent_descend, leaf_far, leaf_descend, out_basis, out, values, sem
):
    block = picked(lambda j: tops[top_rows[0, j]], 16)
    top_field = dot(block, top_coupling[0].reshape(1024, 64)).astype(BF16)
    column = lax.broadcasted_iota(jnp.int32, (32, 256), 1)
    parents = [(parent_far[q] + dot(top_field, parent_descend[q])).astype(BF16) for q in range(PARENT)]
    copies = []
    for q in range(PARENT):
        for b in range(q * 8, q * 8 + 8):
            field = (leaf_far[b] + dot(parents[q], leaf_descend[b])).astype(BF16)
            value = dot(field, out_basis[b])
            values[b] = jnp.where(column < counts[b], value, jnp.zeros_like(value)).astype(BF16)
        part = pl.ds(q * 8, 8)
        copies.append(pltpu.make_async_copy(values.at[part], out.at[part], sem.at[q]))
        copies[q].start()
    for copy in copies:
        copy.wait()


def down(counts, top_rows, *operands):
    smem, vmem = pl.BlockSpec(memory_space=pltpu.SMEM), pl.BlockSpec(memory_space=pltpu.VMEM)
    return pl.pallas_call(
        down_kernel,
        in_specs=[smem] * 2 + [vmem] * len(operands),
        out_specs=pl.BlockSpec(memory_space=pltpu.HBM),
        out_shape=jax.ShapeDtypeStruct((64, 32, 256), BF16),
        scratch_shapes=[pltpu.VMEM((64, 32, 256), BF16), pltpu.SemaphoreType.DMA((PARENT,))],
        compiler_params=pltpu.CompilerParams(vmem_limit_bytes=4 * MIB),
        cost_estimate=pl.CostEstimate(flops=2 * 64 * 32 * 64 * 320, bytes_accessed=6 * MIB, transcendentals=0),
        name="down",
    )(counts, top_rows, *operands)


def body(
    charges,
    counts,
    leaf_basis,
    out_basis,
    leaf_transfer,
    leaf_descend,
    parent_transfer,
    parent_descend,
    leaf_coupling,
    far_owner,
    far_local,
    parent_coupling,
    parent_owner,
    parent_index,
    top_coupling,
    top_source,
):
    x, y, z, c = (lax.axis_index(a) for a in "xyzc")
    place = jnp.stack([x, y, z, c]).astype(jnp.int32)
    place, charges = lax.optimization_barrier((place, charges))

    hbm = lambda a: pltpu.with_memory_space_constraint(a, pltpu.HBM)
    coeffs = up(*map(hbm, (counts, charges, leaf_basis, leaf_transfer, parent_transfer)))
    names = (far_owner.T, far_local.T, parent_owner, parent_index, top_source)
    early, late, prepared, more = gather(coeffs, stage(place, *names, leaf_coupling, STAGED), stage_more(leaf_coupling))
    head, leaf_rows, parent_rows, top_rows = prepared
    swap = lambda pieces: [(other_core(piece), 16 + first) for piece, first in pieces]
    gathered = assemble(early + swap(early))
    gathered = assemble(late + swap(late), gathered)
    tops = column_tops(early + late)
    planes = [tops] + [lax.ppermute(tops, "x", [(i, i ^ m) for i in range(4)]) for m in (1, 2, 3)]

    leaf_far, parent_staged = couple(leaf_rows, gathered, head, more, leaf_coupling, parent_coupling)
    planes, leaf_far = lax.optimization_barrier((planes, leaf_far))
    tops = jnp.concatenate(planes)
    tops = jnp.concatenate([tops, other_core(tops)])
    parent_far = couple_parents(parent_rows, gathered, parent_staged)
    return down(
        counts, top_rows, tops, top_coupling, parent_far, parent_descend, leaf_far, leaf_descend, out_basis
    )


def solution(mesh):
    fine = Mesh(mesh.devices.reshape(4, 4, 4, 2), ("x", "y", "z", "c"))
    spec = P(("x", "y", "z", "c"))
    return jax.shard_map(body, mesh=fine, in_specs=(spec,) * 16, out_specs=spec, check_vma=False)
```

```python
import functools

import jax
import jax.numpy as jnp
from jax import lax
from jax.experimental import pallas as pl
from jax.experimental.pallas import tpu as pltpu
from jax.sharding import Mesh
from jax.sharding import PartitionSpec as P

BF16 = jnp.bfloat16
F32 = jnp.float32
LEAF, PARENT = 64, 8
ROWS = LEAF + PARENT + 1
MORE = 16
NT = (((1,), (1,)), ((), ()))
MIB = 1 << 20


def dot(a, b):
    return jnp.dot(a, b, preferred_element_type=F32)


def pack(c):
    return jnp.concatenate([c[:16], c[16:]], axis=1)


def up_kernel(counts, charges, basis, transfer, parent_transfer, out, live, charge, base, move, lift, sem):
    chunks = 2
    size = LEAF // chunks
    count_copy = pltpu.make_async_copy(counts, live, sem.at[0])
    count_copy.start()
    copies = []
    for k in range(chunks):
        part = pl.ds(k * size, size)
        copies.append(
            [
                pltpu.make_async_copy(charges.at[part], charge.at[part], sem.at[3 + 2 * k]),
                pltpu.make_async_copy(basis.at[part], base.at[part], sem.at[4 + 2 * k]),
            ]
        )
        for copy in copies[k]:
            copy.start()
    transfers = [
        pltpu.make_async_copy(transfer, move, sem.at[1]),
        pltpu.make_async_copy(parent_transfer, lift, sem.at[2]),
    ]
    for copy in transfers:
        copy.start()
    count_copy.wait()
    column = lax.broadcasted_iota(jnp.int32, (32, 256), 1)
    coeffs = []
    for k in range(chunks):
        for copy in copies[k]:
            copy.wait()
        for b in range(k * size, (k + 1) * size):
            masked = jnp.where(column < live[b], charge[b], jnp.zeros((32, 256), BF16))
            coeff = lax.dot_general(masked, base[b], NT, preferred_element_type=F32).astype(BF16)
            out[b] = pack(coeff)
            coeffs.append(coeff)
    for copy in transfers:
        copy.wait()
    parents = []
    for q in range(PARENT):
        family = jnp.concatenate(coeffs[q * 8 : q * 8 + 8], axis=1)
        parents.append(dot(family, move[q * 8 : q * 8 + 8].reshape(512, 64)).astype(BF16))
        out[LEAF + q] = pack(parents[q])
    top = dot(jnp.concatenate(parents, axis=1), lift[...].reshape(512, 64))
    out[ROWS - 1] = pack(top.astype(BF16))


def up(*operands):
    hbm = pl.BlockSpec(memory_space=pltpu.HBM)
    return pl.pallas_call(
        up_kernel,
        in_specs=[hbm] * 5,
        out_specs=pl.BlockSpec(memory_space=pltpu.VMEM),
        out_shape=jax.ShapeDtypeStruct((ROWS, 16, 128), BF16),
        scratch_shapes=[pltpu.SMEM((LEAF,), jnp.int32)]
        + [pltpu.VMEM(x.shape, BF16) for x in operands[1:]]
        + [pltpu.SemaphoreType.DMA((7,))],
        compiler_params=pltpu.CompilerParams(vmem_limit_bytes=8 * MIB),
        cost_estimate=pl.CostEstimate(flops=2 * 64 * 32 * 64 * 320, bytes_accessed=5 * MIB, transcendentals=0),
        name="up",
    )(*operands)


def pairs(second, mask):
    out = []
    for y in range(4):
        for z in range(4):
            for c in range(2):
                along_y = (c == 0) != second
                ty, tz = (y ^ mask, z) if along_y else (y, z ^ mask)
                out.append(((y * 4 + z) * 2 + c, (ty * 4 + tz) * 2 + c))
    return out


def send(x, second, mask):
    return lax.ppermute(x, ("y", "z", "c"), pairs(second, mask))


def other_core(x):
    return lax.ppermute(x, "c", [(0, 1), (1, 0)])


def gather(s, staged, more):
    s = s[None]
    a, o, b = (send(s, False, m) for m in (1, 2, 3))
    near, far = jnp.concatenate([s, a]), jnp.concatenate([o, b])
    far, staged = lax.optimization_barrier((far, staged))
    near_a, near_b = send(near, True, 1), send(near, True, 3)
    far_a, far_b = send(far, True, 1), send(far, True, 3)
    near_b, more = lax.optimization_barrier((near_b, more))
    near_o, far_o = send(near_a, True, 3), send(far_b, True, 1)
    early = [(near, 0), (far, 2), (near_a, 4), (far_a, 6), (near_b, 12), (far_b, 14)]
    return early, [(near_o, 8), (far_o, 10)], staged, more


def place_kernel(firsts, *refs):
    out = refs[-1]
    for ref, first in zip(refs, firsts):
        for i in range(2):
            out[(first + i) * ROWS : (first + i + 1) * ROWS] = ref[i]


def assemble(pieces, *earlier):
    vmem = pl.BlockSpec(memory_space=pltpu.VMEM)
    n = len(pieces)
    return pl.pallas_call(
        functools.partial(place_kernel, [first for _, first in pieces]),
        in_specs=[vmem] * (n + len(earlier)),
        out_specs=vmem,
        out_shape=jax.ShapeDtypeStruct((32 * ROWS, 16, 128), BF16),
        input_output_aliases={n: 0} if earlier else {},
        compiler_params=pltpu.CompilerParams(vmem_limit_bytes=10 * MIB),
        cost_estimate=pl.CostEstimate(flops=0, bytes_accessed=4096, transcendentals=0),
        name="assemble",
    )(*[x for x, _ in pieces], *earlier)


def tops_kernel(firsts, *refs):
    n = len(firsts)
    out, sem = refs[n:]
    copies = []
    for ref, first in zip(refs[:n], firsts):
        for i in range(2):
            copies.append(pltpu.make_async_copy(ref.at[i, ROWS - 1], out.at[first + i], sem.at[len(copies)]))
            copies[-1].start()
    for copy in copies:
        copy.wait()


def column_tops(pieces):
    n = len(pieces)
    return pl.pallas_call(
        functools.partial(tops_kernel, [first for _, first in pieces]),
        in_specs=[pl.BlockSpec(memory_space=pltpu.HBM)] * n,
        out_specs=pl.BlockSpec(memory_space=pltpu.VMEM),
        out_shape=jax.ShapeDtypeStruct((16, 16, 128), BF16),
        scratch_shapes=[pltpu.SemaphoreType.DMA((2 * n,))],
        compiler_params=pltpu.CompilerParams(vmem_limit_bytes=4 * MIB),
        cost_estimate=pl.CostEstimate(flops=0, bytes_accessed=4096, transcendentals=0),
        name="tops",
    )(*[x for x, _ in pieces])


def slots(owner, y, z, c):
    oy, oz, oc = owner // 8, owner // 2 % 4, owner % 2
    ry, rz = oy ^ y, oz ^ z
    return (oc ^ c) * 16 + jnp.where(oc == 0, rz * 4 + ry, ry * 4 + rz)


def picked(load, entries):
    lane = lax.broadcasted_iota(jnp.int32, (16, 128), 1) < 64
    low, high = [], []
    for j in range(0, entries, 2):
        a, b = load(j), load(j + 1)
        low.append(jnp.where(lane, a, jnp.concatenate([b[:, 64:], b[:, :64]], axis=1)))
        high.append(jnp.where(lane, jnp.concatenate([a[:, 64:], a[:, :64]], axis=1), b))
    return jnp.concatenate([jnp.concatenate(low, axis=1), jnp.concatenate(high, axis=1)], axis=0)


CHUNK = 8
STAGED = 16


def stage_kernel(place, *refs):
    names, coupling, head, leaf_rows, parent_rows, top_rows = refs[:5], refs[5], *refs[6:10]
    held, sem = refs[10:15], refs[15]
    reads = [pltpu.make_async_copy(src, dst, sem.at[i]) for i, (src, dst) in enumerate(zip(names, held))]
    parts = 4
    size = head.shape[0] // parts
    copies = []
    for k in range(parts):
        part = pl.ds(k * size, size)
        copies.append(pltpu.make_async_copy(coupling.at[part], head.at[part], sem.at[5 + k]))
    for copy in reads + copies:
        copy.start()
    for copy in reads:
        copy.wait()
    x, y, z, c = (place[i] for i in range(4))
    far_owner, far_local, parent_owner, parent_index, source = (ref[...] for ref in held)
    leaf_rows[...] = slots(far_owner, y, z, c) * ROWS + far_local
    parent_rows[...] = slots(parent_owner, y, z, c) * ROWS + LEAF + parent_index
    slot = slots(source % 32, y, z, c)
    top_rows[...] = slot // 16 * 64 + ((source // 32) ^ x) * 16 + slot % 16
    for copy in copies:
        copy.wait()


def stage(place, far_owner, far_local, parent_owner, parent_index, top_source, coupling, count):
    smem, vmem = pl.BlockSpec(memory_space=pltpu.SMEM), pl.BlockSpec(memory_space=pltpu.VMEM)
    names = (far_owner, far_local, parent_owner, parent_index, top_source)
    hbm = lambda a: pltpu.with_memory_space_constraint(a, pltpu.HBM)
    return pl.pallas_call(
        stage_kernel,
        in_specs=[smem] + [pl.BlockSpec(memory_space=pltpu.HBM)] * 6,
        out_specs=[vmem] * 4,
        out_shape=[jax.ShapeDtypeStruct((count,) + coupling.shape[1:], BF16)]
        + [jax.ShapeDtypeStruct(x.shape, jnp.int32) for x in (far_owner, parent_owner, top_source)],
        scratch_shapes=[pltpu.VMEM(x.shape, jnp.int32) for x in names] + [pltpu.SemaphoreType.DMA((9,))],
        compiler_params=pltpu.CompilerParams(vmem_limit_bytes=2 * MIB),
        cost_estimate=pl.CostEstimate(flops=0, bytes_accessed=4096, transcendentals=0),
        name="stage",
    )(place, *map(hbm, names), hbm(coupling))


def stage_more_kernel(coupling, out, sem):
    parts = 4
    size = out.shape[0] // parts
    copies = []
    for k in range(parts):
        source = coupling.at[pl.ds(STAGED + k * size, size)]
        copies.append(pltpu.make_async_copy(source, out.at[pl.ds(k * size, size)], sem.at[k]))
        copies[k].start()
    for copy in copies:
        copy.wait()


def stage_more(coupling):
    return pl.pallas_call(
        stage_more_kernel,
        in_specs=[pl.BlockSpec(memory_space=pltpu.HBM)],
        out_specs=pl.BlockSpec(memory_space=pltpu.VMEM),
        out_shape=jax.ShapeDtypeStruct((MORE,) + coupling.shape[1:], BF16),
        scratch_shapes=[pltpu.SemaphoreType.DMA((4,))],
        compiler_params=pltpu.CompilerParams(vmem_limit_bytes=2 * MIB),
        cost_estimate=pl.CostEstimate(flops=0, bytes_accessed=4096, transcendentals=0),
        name="stage_more",
    )(pltpu.with_memory_space_constraint(coupling, pltpu.HBM))


def couple_kernel(
    leaf_rows, gathered, head, more, coupling, parent_coupling, leaf_far, parent_staged, staged, leaf_named, chunk_sem, row_sem
):
    chunks = []
    for k in range((LEAF - STAGED - MORE) // CHUNK):
        source = coupling.at[pl.ds(STAGED + MORE + k * CHUNK, CHUNK)]
        chunks.append(pltpu.make_async_copy(source, staged.at[pl.ds(k * CHUNK, CHUNK)], chunk_sem.at[k]))
    chunks.append(pltpu.make_async_copy(parent_coupling, parent_staged, chunk_sem.at[len(chunks)]))
    named = pltpu.make_async_copy(leaf_rows, leaf_named, row_sem)
    for copy in [named] + chunks:
        copy.start()
    named.wait()
    for b in range(STAGED):
        block = picked(lambda j: gathered[leaf_named[j, b]], 16)
        leaf_far[b] = dot(block, head[b].reshape(1024, 64))
    for i in range(MORE):
        block = picked(lambda j: gathered[leaf_named[j, STAGED + i]], 16)
        leaf_far[STAGED + i] = dot(block, more[i].reshape(1024, 64))
    for k in range((LEAF - STAGED - MORE) // CHUNK):
        chunks[k].wait()
        for i in range(k * CHUNK, (k + 1) * CHUNK):
            block = picked(lambda j: gathered[leaf_named[j, STAGED + MORE + i]], 16)
            leaf_far[STAGED + MORE + i] = dot(block, staged[i].reshape(1024, 64))
    chunks[-1].wait()


def couple_parents_kernel(parent_rows, gathered, coupling, far, named, sem):
    copy = pltpu.make_async_copy(parent_rows, named, sem)
    copy.start()
    copy.wait()
    for q in range(PARENT):
        block = picked(lambda j: gathered[named[q, j]], 16)
        far[q] = dot(block, coupling[q].reshape(1024, 64))


def couple_parents(parent_rows, gathered, coupling):
    vmem = pl.BlockSpec(memory_space=pltpu.VMEM)
    return pl.pallas_call(
        couple_parents_kernel,
        in_specs=[vmem] * 3,
        out_specs=vmem,
        out_shape=jax.ShapeDtypeStruct((PARENT, 32, 64), F32),
        scratch_shapes=[pltpu.SMEM(parent_rows.shape, jnp.int32), pltpu.SemaphoreType.DMA],
        compiler_params=pltpu.CompilerParams(vmem_limit_bytes=4 * MIB),
        cost_estimate=pl.CostEstimate(flops=2 * 8 * 32 * 64 * 1024, bytes_accessed=3 * MIB, transcendentals=0),
        name="couple_parents",
    )(parent_rows, gathered, coupling)


def couple(leaf_rows, gathered, head, more, coupling, parent_coupling):
    vmem = pl.BlockSpec(memory_space=pltpu.VMEM)
    return pl.pallas_call(
        couple_kernel,
        in_specs=[vmem] * 4 + [pl.BlockSpec(memory_space=pltpu.HBM)] * 2,
        out_specs=[vmem, vmem],
        out_shape=[jax.ShapeDtypeStruct((LEAF, 32, 64), F32), jax.ShapeDtypeStruct(parent_coupling.shape, BF16)],
        scratch_shapes=[
            pltpu.VMEM((LEAF - STAGED - MORE,) + coupling.shape[1:], BF16),
            pltpu.SMEM(leaf_rows.shape, jnp.int32),
            pltpu.SemaphoreType.DMA(((LEAF - STAGED - MORE) // CHUNK + 1,)),
            pltpu.SemaphoreType.DMA,
        ],
        compiler_params=pltpu.CompilerParams(vmem_limit_bytes=18 * MIB),
        cost_estimate=pl.CostEstimate(flops=2 * 72 * 32 * 64 * 1024, bytes_accessed=28 * MIB, transcendentals=0),
        name="couple",
    )(
        leaf_rows,
        gathered,
        head,
        more,
        pltpu.with_memory_space_constraint(coupling, pltpu.HBM),
        pltpu.with_memory_space_constraint(parent_coupling, pltpu.HBM),
    )


def down_kernel(
    count_source, row_source, tops, top_coupling, parent_far, parent_descend, leaf_far, leaf_descend, out_basis, out, values, counts, top_rows, sem
):
    row_copy = pltpu.make_async_copy(row_source, top_rows, sem.at[PARENT])
    count_copy = pltpu.make_async_copy(count_source, counts, sem.at[PARENT + 1])
    row_copy.start()
    count_copy.start()
    row_copy.wait()
    count_copy.wait()
    block = picked(lambda j: tops[top_rows[0, j]], 16)
    top_field = dot(block, top_coupling[0].reshape(1024, 64)).astype(BF16)
    column = lax.broadcasted_iota(jnp.int32, (32, 256), 1)
    parents = [(parent_far[q] + dot(top_field, parent_descend[q])).astype(BF16) for q in range(PARENT)]
    copies = []
    for q in range(PARENT):
        for b in range(q * 8, q * 8 + 8):
            field = (leaf_far[b] + dot(parents[q], leaf_descend[b])).astype(BF16)
            value = dot(field, out_basis[b])
            values[b] = jnp.where(column < counts[b], value, jnp.zeros_like(value)).astype(BF16)
        part = pl.ds(q * 8, 8)
        copies.append(pltpu.make_async_copy(values.at[part], out.at[part], sem.at[q]))
        copies[q].start()
    for copy in copies:
        copy.wait()


def down(counts, top_rows, *operands):
    hbm, vmem = pl.BlockSpec(memory_space=pltpu.HBM), pl.BlockSpec(memory_space=pltpu.VMEM)
    return pl.pallas_call(
        down_kernel,
        in_specs=[hbm, vmem] + [vmem] * len(operands),
        out_specs=pl.BlockSpec(memory_space=pltpu.HBM),
        out_shape=jax.ShapeDtypeStruct((64, 32, 256), BF16),
        scratch_shapes=[
            pltpu.VMEM((64, 32, 256), BF16),
            pltpu.SMEM(counts.shape, jnp.int32),
            pltpu.SMEM(top_rows.shape, jnp.int32),
            pltpu.SemaphoreType.DMA((PARENT + 2,)),
        ],
        compiler_params=pltpu.CompilerParams(vmem_limit_bytes=4 * MIB),
        cost_estimate=pl.CostEstimate(flops=2 * 64 * 32 * 64 * 320, bytes_accessed=6 * MIB, transcendentals=0),
        name="down",
    )(pltpu.with_memory_space_constraint(counts, pltpu.HBM), top_rows, *operands)


def body(
    charges,
    counts,
    leaf_basis,
    out_basis,
    leaf_transfer,
    leaf_descend,
    parent_transfer,
    parent_descend,
    leaf_coupling,
    far_owner,
    far_local,
    parent_coupling,
    parent_owner,
    parent_index,
    top_coupling,
    top_source,
):
    x, y, z, c = (lax.axis_index(a) for a in "xyzc")
    place = jnp.stack([x, y, z, c]).astype(jnp.int32)
    place, charges = lax.optimization_barrier((place, charges))

    hbm = lambda a: pltpu.with_memory_space_constraint(a, pltpu.HBM)
    coeffs = up(*map(hbm, (counts, charges, leaf_basis, leaf_transfer, parent_transfer)))
    names = (far_owner.T, far_local.T, parent_owner, parent_index, top_source)
    early, late, prepared, more = gather(coeffs, stage(place, *names, leaf_coupling, STAGED), stage_more(leaf_coupling))
    head, leaf_rows, parent_rows, top_rows = prepared
    swap = lambda pieces: [(other_core(piece), 16 + first) for piece, first in pieces]
    gathered = assemble(early + swap(early))
    gathered = assemble(late + swap(late), gathered)
    tops = column_tops(early + late)
    planes = [tops] + [lax.ppermute(tops, "x", [(i, i ^ m) for i in range(4)]) for m in (1, 2, 3)]

    leaf_far, parent_staged = couple(leaf_rows, gathered, head, more, leaf_coupling, parent_coupling)
    planes, leaf_far = lax.optimization_barrier((planes, leaf_far))
    tops = jnp.concatenate(planes)
    tops = jnp.concatenate([tops, other_core(tops)])
    parent_far = couple_parents(parent_rows, gathered, parent_staged)
    return down(
        counts, top_rows, tops, top_coupling, parent_far, parent_descend, leaf_far, leaf_descend, out_basis
    )


def solution(mesh):
    fine = Mesh(mesh.devices.reshape(4, 4, 4, 2), ("x", "y", "z", "c"))
    spec = P(("x", "y", "z", "c"))
    return jax.shard_map(body, mesh=fine, in_specs=(spec,) * 16, out_specs=spec, check_vma=False)
```
